512 devices in a mesh: grp: 32 (over y, z_lo), tp: 16 (over x, z_hi, core).
Axes of the slice: x: 4, y: 8, z: 8 (z_hi: 2, z_lo: 4; z = z_hi * 4 + z_lo), core: 2. Of those that a mesh axis runs over, the one named last changes fastest.
Arguments:
- trainer_token_inputs: bfloat16 [8192, 16384], P('grp', 'tp'), may hold values from -6 to 6
- weighted_output_cotangents: bfloat16 [2, 512, 8192], P(None, 'tp', 'grp'), may hold values from -0.049804688 to 0.049804688
- adapter_down_master: float32 [2, 64, 16384], P(None, 'grp', 'tp'), may hold values from -0.046875 to 0.046875
- adapter_up_master: float32 [2, 512, 64], P(None, 'tp', 'grp'), may hold values from -0.4 to 0.4
- down_first_moment: float32 [2, 64, 16384], P(None, 'grp', 'tp'), may hold values from -0.3 to 0.3
- down_second_moment: float32 [2, 64, 16384], P(None, 'grp', 'tp'), may hold values from 0.01 to 0.2
- up_first_moment: float32 [2, 512, 64], P(None, 'tp', 'grp'), may hold values from -0.3 to 0.3
- up_second_moment: float32 [2, 512, 64], P(None, 'tp', 'grp'), may hold values from 0.01 to 0.2
- frozen_weights: bfloat16 [2, 16384, 512], P(None, 'tp'), may hold values from -0.046875 to 0.046875
- decode_step_inputs: bfloat16 [1024, 4, 16384], P('grp', None, 'tp'), may hold values from -6 to 6
- queries: bfloat16 [1024, 4, 8192], P(('grp', 'tp')), may hold values from -150 to 150
- rotated_key_cache: bfloat16 [1024, 4, 256, 128], P(('grp', 'tp')), may hold values from -5 to 5
- stored_value_cache: bfloat16 [1024, 4, 256, 128], P(('grp', 'tp')), may hold values from -6 to 6
- lengths: int32 [1024], P(('grp', 'tp')), may hold values from 64 to 256
Outputs:
- attended: float32 [1024, 4, 8192], P(('grp', 'tp'))
- new_keys: float32 [1024, 4, 512], P(('grp', 'tp'))
- new_values: float32 [1024, 4, 512], P(('grp', 'tp'))
- fresh_down_factors: float32 [2, 64, 16384], P(None, 'grp', 'tp')
- fresh_up_factors: float32 [2, 512, 64], P(None, 'tp', 'grp')
- fresh_down_first_moment: float32 [2, 64, 16384], P(None, 'grp', 'tp')
- fresh_down_second_moment: float32 [2, 64, 16384], P(None, 'grp', 'tp')
- fresh_up_first_moment: float32 [2, 512, 64], P(None, 'tp', 'grp')
- fresh_up_second_moment: float32 [2, 512, 64], P(None, 'tp', 'grp')
The draws below stay inside these ranges and needn't reach their ends.
All inputs are finite; a program needn't handle non-finite values.
Results may differ from the reference program's by a relative error of at most 0.008.
Values may be sent and summed in bfloat16 or wider, within the bound.
No kernel may reach another device: no remote copies, remote signals or barrier semaphores. Data moves between devices by JAX's collectives and lax.ppermute only.
A program may use at most 64 MiB of HBM per device.

```python
import math
import jax
import jax.numpy as jnp
from jax import lax

MODEL_WIDTH = 16384
HEAD = 128
KV_HEADS = 4
Q_HEADS = 64
ADAPTER_RANK = 64
STEPS = 4
OPT_STEP = 20
ROWS_DEV = 2
CACHE = 256
KEY_VALUE_WIDTH = 512
GROUP = 16
TRAIN_TOKENS = 8192
ROWS = 1024
N_TP = 16


def cache_head(key):
    head_zero = jnp.clip(jax.random.normal(jax.random.fold_in(key, 71), (ROWS, CACHE, HEAD), jnp.float32), -5.0, 5.0)
    return head_zero


def draw_rotated_key_cache(key, part):
    head_zero = cache_head(key)
    key = jax.random.fold_in(key, 3)
    others = jnp.clip(jax.random.normal(key, (ROWS, KV_HEADS - 1, CACHE, HEAD), jnp.float32), -5.0, 5.0)
    return jnp.concatenate([head_zero[:, None], others], axis=1).astype(jnp.bfloat16)


def draw_queries(key, part):
    key = jax.random.fold_in(key, 5)
    values = jnp.clip(jax.random.normal(key, (ROWS, STEPS, Q_HEADS * HEAD), jnp.float32), -5.0, 5.0)
    return values.astype(jnp.bfloat16)


def draw_lengths(key, part):
    key = jax.random.fold_in(key, 7)
    drawn_lengths = jax.random.randint(key, (ROWS,), CACHE // 4, CACHE + 1)
    chosen = jax.random.randint(jax.random.fold_in(key, 1), (), 0, ROWS)
    return jnp.where(jnp.arange(ROWS) == chosen, CACHE, drawn_lengths).astype(jnp.int32)


def level_of(stream_key, extent, pieces, low, top_value):
    gain, own = 1.0, jax.random.fold_in(stream_key, 6)
    for axis_at, parts in pieces:
        steps = jnp.exp(jax.random.uniform(jax.random.fold_in(own, axis_at), (parts,), jnp.float32, low / len(pieces), top_value / len(pieces)))
        gain = gain * jnp.repeat(steps, extent[axis_at] // parts).reshape([-1 if axis == axis_at else 1 for axis in range(len(extent))])
    return gain


def gaussian(stream_key, shape, scale, reach, shards=(), kind=jnp.bfloat16):
    drawn = jax.random.normal(stream_key, shape, jnp.float32) * scale
    if len(shards) > 0:
        drawn = level_of(stream_key, shape, shards, -0.22, 0.18) * drawn
    return jnp.clip(drawn, min=-reach, max=reach).astype(kind)


def setup_inputs(seed: int = 0) -> dict:
    splits = jax.random.split(jax.random.key(seed), 15)
    trainer_token_inputs = gaussian(splits[0], (TRAIN_TOKENS, MODEL_WIDTH), 1.0, 6.0, ((0, 32), (1, 16)))
    weighted_output_cotangents = gaussian(splits[1], (2, KEY_VALUE_WIDTH, TRAIN_TOKENS), 0.0078125, 0.049804688, ((1, 16), (2, 32)))
    adapter_down_master = gaussian(splits[2], (2, ADAPTER_RANK, MODEL_WIDTH), MODEL_WIDTH ** -0.5, 0.046875, ((1, 32), (2, 16)), jnp.float32)
    adapter_up_master = gaussian(splits[3], (2, KEY_VALUE_WIDTH, ADAPTER_RANK), 0.0625, 0.4, ((1, 16), (2, 32)), jnp.float32)
    down_first_moment = gaussian(splits[4], (2, ADAPTER_RANK, MODEL_WIDTH), 0.05, 0.3, ((1, 32), (2, 16)), jnp.float32)
    down_second_moment = jnp.clip(jnp.exp(math.log(0.2) - 2.9957323 * jax.random.uniform(splits[5], (2, ADAPTER_RANK, MODEL_WIDTH), jnp.float32) ** level_of(splits[5], (2, ADAPTER_RANK, MODEL_WIDTH), ((1, 32), (2, 16)), -0.2, 0.2)), 0.01, 0.2)
    up_first_moment = gaussian(splits[6], (2, KEY_VALUE_WIDTH, ADAPTER_RANK), 0.05, 0.3, ((1, 16), (2, 32)), jnp.float32)
    up_second_moment = jnp.clip(jnp.exp(math.log(0.2) - 2.9957323 * jax.random.uniform(splits[7], (2, KEY_VALUE_WIDTH, ADAPTER_RANK), jnp.float32) ** level_of(splits[7], (2, KEY_VALUE_WIDTH, ADAPTER_RANK), ((1, 16), (2, 32)), -0.2, 0.2)), 0.01, 0.2)
    frozen_weights = gaussian(splits[8], (2, MODEL_WIDTH, KEY_VALUE_WIDTH), MODEL_WIDTH ** -0.5, 0.046875, ((1, 16),))
    decode_step_inputs = gaussian(splits[9], (ROWS, STEPS, MODEL_WIDTH), 1.0, 6.0, ((0, 32), (2, 16)))
    queries = draw_queries(jax.random.fold_in(splits[14], 71), 0)
    rotated_key_cache = draw_rotated_key_cache(jax.random.fold_in(splits[14], 71), 0)
    stored_value_cache = gaussian(splits[12], (ROWS, KV_HEADS, CACHE, HEAD), 1.0, 6.0, ((0, 512),))
    lengths = draw_lengths(jax.random.fold_in(splits[14], 71), 0)
    return {"trainer_token_inputs": trainer_token_inputs, "weighted_output_cotangents": weighted_output_cotangents, "adapter_down_master": adapter_down_master, "adapter_up_master": adapter_up_master, "down_first_moment": down_first_moment, "down_second_moment": down_second_moment, "up_first_moment": up_first_moment, "up_second_moment": up_second_moment, "frozen_weights": frozen_weights, "decode_step_inputs": decode_step_inputs, "queries": queries, "rotated_key_cache": rotated_key_cache, "stored_value_cache": stored_value_cache, "lengths": lengths}


ADAPTER_SCALE = 2.0
LEARN_RATE = 0.001
WEIGHT_DECAY = 0.01
BETA_FIRST = 0.9
BETA_SECOND = 0.95
EPSILON = 1e-08
THETA = 500000.0
ROPE_FACTOR = 8.0
LOW_FACTOR = 1.0
HIGH_FACTOR = 4.0
INITIAL_CONTEXT = 8192.0
MASKED = -1e+30

def rope_frequencies(head_size):
    half_head = head_size // 2
    exponent = jnp.arange(half_head, dtype=jnp.float32) * (2.0 / head_size)
    base_frequency = jnp.power(jnp.float32(THETA), -exponent)
    wavelength = 2.0 * math.pi / base_frequency
    smooth = (INITIAL_CONTEXT / wavelength - LOW_FACTOR) / (HIGH_FACTOR - LOW_FACTOR)
    blended = (1.0 - smooth) * base_frequency / ROPE_FACTOR + smooth * base_frequency
    scaled = jnp.where(wavelength > INITIAL_CONTEXT / LOW_FACTOR, base_frequency / ROPE_FACTOR, blended)
    return jnp.where(wavelength < INITIAL_CONTEXT / HIGH_FACTOR, base_frequency, scaled)

def rotate_keys(vectors, positions):
    half_head = vectors.shape[-1] // 2
    frequency = rope_frequencies(vectors.shape[-1])
    angles = positions.astype(jnp.float32)[..., None] * frequency
    cosine = jnp.cos(angles)[..., None, :]
    sine_part = jnp.sin(angles)[..., None, :]
    first_half = vectors[..., :half_head]
    second_half = vectors[..., half_head:]
    return jnp.concatenate([first_half * cosine - second_half * sine_part, second_half * cosine + first_half * sine_part], axis=-1)

def optimizer_update(current, gradient, moment_mean, moment_square):
    mean_next = BETA_FIRST * moment_mean + (1.0 - BETA_FIRST) * gradient
    square_next = BETA_SECOND * moment_square + (1.0 - BETA_SECOND) * gradient * gradient
    bias_first = 1.0 - BETA_FIRST ** OPT_STEP
    bias_second = 1.0 - BETA_SECOND ** OPT_STEP
    update = mean_next / bias_first / (jnp.sqrt(square_next / bias_second) + EPSILON)
    return (current - LEARN_RATE * (update + WEIGHT_DECAY * current), mean_next, square_next)

def attend_group(block):
    query_block, key_block, value_block, fresh_keys, fresh_values, length_block = block
    row_count = query_block.shape[0]
    scaling = 1.0 / math.sqrt(HEAD)
    query_heads = query_block.astype(jnp.float32).reshape(row_count, STEPS, KV_HEADS, GROUP, HEAD)
    cache_scores = jnp.einsum('rtghe,rgpe->rtghp', query_heads, key_block.astype(jnp.float32)) * scaling
    valid = jnp.arange(CACHE, dtype=jnp.int32)[None, :] < length_block[:, None]
    cache_scores = jnp.where(valid[:, None, None, None, :], cache_scores, MASKED)
    fresh_heads = fresh_keys.astype(jnp.float32).reshape(row_count, STEPS, KV_HEADS, HEAD)
    fresh_scores = jnp.einsum('rtghe,rsge->rtghs', query_heads, fresh_heads) * scaling
    causal = jnp.arange(STEPS)[:, None] >= jnp.arange(STEPS)[None, :]
    fresh_scores = jnp.where(causal[None, :, None, None, :], fresh_scores, MASKED)
    scores = jnp.concatenate([cache_scores, fresh_scores], axis=-1)
    peak_score = lax.optimization_barrier(jnp.max(scores, axis=-1, keepdims=True))
    exponent = jnp.exp(scores - peak_score)
    weights = (exponent / lax.optimization_barrier(jnp.sum(exponent, axis=-1, keepdims=True))).astype(jnp.bfloat16)
    fresh_value_heads = fresh_values.astype(jnp.float32).reshape(row_count, STEPS, KV_HEADS, HEAD)
    result = jnp.einsum('rtghp,rgpe->rtghe', weights[..., :CACHE].astype(jnp.float32), value_block.astype(jnp.float32))
    result = result + jnp.einsum('rtghs,rsge->rtghe', weights[..., CACHE:].astype(jnp.float32), fresh_value_heads)
    return result.reshape(row_count, STEPS, Q_HEADS * HEAD)

def reference(trainer_token_inputs, weighted_output_cotangents, adapter_down_master, adapter_up_master, down_first_moment, down_second_moment, up_first_moment, up_second_moment, frozen_weights, decode_step_inputs, queries, rotated_key_cache, stored_value_cache, lengths):
    bfloat_down_factors = adapter_down_master.astype(jnp.bfloat16)
    bfloat_up_factors = adapter_up_master.astype(jnp.bfloat16)
    down_gradients = []
    up_gradients = []
    for group_member in range(2):
        projected_rows = jnp.dot(trainer_token_inputs, bfloat_down_factors[group_member].T, preferred_element_type=jnp.float32).astype(jnp.bfloat16)
        gathered_rows = jnp.dot(weighted_output_cotangents[group_member].T, bfloat_up_factors[group_member], preferred_element_type=jnp.float32).astype(jnp.bfloat16)
        down_gradients.append(ADAPTER_SCALE * jnp.dot(gathered_rows.T, trainer_token_inputs, preferred_element_type=jnp.float32))
        up_gradients.append(ADAPTER_SCALE * jnp.dot(weighted_output_cotangents[group_member], projected_rows, preferred_element_type=jnp.float32))
    down_gradient = jnp.stack(down_gradients)
    up_gradient = jnp.stack(up_gradients)
    fresh_down_factors, fresh_down_first_moment, fresh_down_second_moment = optimizer_update(adapter_down_master, down_gradient, down_first_moment, down_second_moment)
    fresh_up_factors, fresh_up_first_moment, fresh_up_second_moment = optimizer_update(adapter_up_master, up_gradient, up_first_moment, up_second_moment)
    merged_weights_list = []
    for group_member in range(2):
        weight_change = jnp.dot(fresh_down_factors[group_member].T, fresh_up_factors[group_member].T, precision=lax.Precision.HIGHEST)
        merged_weights_list.append((frozen_weights[group_member].astype(jnp.float32) + ADAPTER_SCALE * weight_change).astype(jnp.bfloat16))
    flat_inputs = decode_step_inputs.reshape(ROWS * STEPS, MODEL_WIDTH)
    key_raw = jnp.dot(flat_inputs, merged_weights_list[0], preferred_element_type=jnp.float32).reshape(ROWS, STEPS, KV_HEADS, HEAD)
    value_raw = jnp.dot(flat_inputs, merged_weights_list[1], preferred_element_type=jnp.float32).reshape(ROWS, STEPS, KEY_VALUE_WIDTH)
    positions = lengths[:, None] + jnp.arange(STEPS, dtype=jnp.int32)[None, :]
    new_keys = rotate_keys(key_raw, positions).reshape(ROWS, STEPS, KEY_VALUE_WIDTH)
    new_values = value_raw
    key_entries = lax.optimization_barrier(new_keys.astype(jnp.bfloat16))
    value_entries = lax.optimization_barrier(new_values.astype(jnp.bfloat16))
    group_rows = ROWS_DEV * N_TP
    groups = ROWS // group_rows
    blocks = (queries.reshape(groups, group_rows, STEPS, Q_HEADS * HEAD), rotated_key_cache.reshape(groups, group_rows, KV_HEADS, CACHE, HEAD), stored_value_cache.reshape(groups, group_rows, KV_HEADS, CACHE, HEAD), key_entries.reshape(groups, group_rows, STEPS, KEY_VALUE_WIDTH), value_entries.reshape(groups, group_rows, STEPS, KEY_VALUE_WIDTH), lengths.reshape(groups, group_rows))
    attended = lax.map(attend_group, blocks).reshape(ROWS, STEPS, Q_HEADS * HEAD)
    return (attended, new_keys, new_values, fresh_down_factors, fresh_up_factors, fresh_down_first_moment, fresh_down_second_moment, fresh_up_first_moment, fresh_up_second_moment)
```

```python
import functools
import math

import jax
import jax.numpy as jnp
from jax import lax
from jax.sharding import PartitionSpec as P

OPT_STEP = 20


ADAPTER_SCALE = 2.0
LEARN_RATE = 0.001
WEIGHT_DECAY = 0.01
BETA_FIRST = 0.9
BETA_SECOND = 0.95
EPSILON = 1e-08
THETA = 500000.0
ROPE_FACTOR = 8.0
LOW_FACTOR = 1.0
HIGH_FACTOR = 4.0
INITIAL_CONTEXT = 8192.0
MASKED = -1e30


def rope_frequencies(head_size):
    half_head = head_size // 2
    exponent = jnp.arange(half_head, dtype=jnp.float32) * (2.0 / head_size)
    base_frequency = jnp.power(jnp.float32(THETA), -exponent)
    wavelength = 2.0 * math.pi / base_frequency
    smooth = (INITIAL_CONTEXT / wavelength - LOW_FACTOR) / (HIGH_FACTOR - LOW_FACTOR)
    blended = (1.0 - smooth) * base_frequency / ROPE_FACTOR + smooth * base_frequency
    scaled = jnp.where(
        wavelength > INITIAL_CONTEXT / LOW_FACTOR, base_frequency / ROPE_FACTOR, blended
    )
    return jnp.where(wavelength < INITIAL_CONTEXT / HIGH_FACTOR, base_frequency, scaled)


def rotate_keys(vectors, positions):
    half_head = vectors.shape[-1] // 2
    frequency = rope_frequencies(vectors.shape[-1])
    angles = positions.astype(jnp.float32)[..., None] * frequency
    cosine = jnp.cos(angles)[..., None, :]
    sine_part = jnp.sin(angles)[..., None, :]
    first_half = vectors[..., :half_head]
    second_half = vectors[..., half_head:]
    return jnp.concatenate(
        [
            first_half * cosine - second_half * sine_part,
            second_half * cosine + first_half * sine_part,
        ],
        axis=-1,
    )


def optimizer_update(current, gradient, moment_mean, moment_square):
    mean_next = BETA_FIRST * moment_mean + (1.0 - BETA_FIRST) * gradient
    square_next = BETA_SECOND * moment_square + (1.0 - BETA_SECOND) * gradient * gradient
    bias_first = 1.0 - BETA_FIRST**OPT_STEP
    bias_second = 1.0 - BETA_SECOND**OPT_STEP
    update = mean_next / bias_first / (jnp.sqrt(square_next / bias_second) + EPSILON)
    return (current - LEARN_RATE * (update + WEIGHT_DECAY * current), mean_next, square_next)


def exchange(pieces, axis):
    return lax.all_to_all(pieces, axis, 0, 0, tiled=True)


def gather_over(block, axis, count):
    return exchange(jnp.broadcast_to(block[None], (count,) + block.shape), axis)


def two_terms(values):
    high = lax.reduce_precision(values, 8, 7)
    return high.astype(jnp.bfloat16), (values - high).astype(jnp.bfloat16)


def product(spec, left, right):
    return jnp.einsum(spec, left, right, preferred_element_type=jnp.float32)


def body(
    groups,
    ranks,
    trainer_token_inputs,
    weighted_output_cotangents,
    adapter_down_master,
    adapter_up_master,
    down_first_moment,
    down_second_moment,
    up_first_moment,
    up_second_moment,
    frozen_weights,
    decode_step_inputs,
    queries,
    rotated_key_cache,
    stored_value_cache,
    lengths,
):
    row_count, steps_count, query_width = queries.shape
    head_groups, cache_slots, head_size = rotated_key_cache.shape[1:]
    kinds, own_rank, own_width = adapter_down_master.shape
    own_columns, tokens = weighted_output_cotangents.shape[1:]
    columns = own_columns * ranks
    own_rows = kinds * own_rank
    all_rows = own_rows * groups
    own_lines = row_count * steps_count
    lanes = 128
    fill = -own_columns % lanes
    is_value = (jnp.arange(all_rows) // own_rank) % kinds == 1

    def own_down(values):
        return values.reshape(own_rows, own_width)

    def own_up(values):
        return values.transpose(0, 2, 1).reshape(own_rows, own_columns)

    def side_by_side(down, up):
        parts = [down.astype(jnp.bfloat16), up.astype(jnp.bfloat16)]
        return jnp.concatenate([parts[0], jnp.pad(parts[1], ((0, 0), (0, fill)))], axis=1)

    def all_factors(down, up):
        both = gather_over(side_by_side(down, up), "grp", groups).reshape(all_rows, -1)
        return both[:, :own_width], both[:, own_width : own_width + own_columns]

    flat_inputs = decode_step_inputs.reshape(-1, own_width)
    frozen_part = [
        product("rd,dc->rc", flat_inputs, frozen_weights[kind]).astype(jnp.bfloat16)
        for kind in range(kinds)
    ]

    down, up = all_factors(own_down(adapter_down_master), own_up(adapter_up_master))
    projected = product("td,nd->tn", trainer_token_inputs, down)
    pulled = product("jct,nc->jtn", weighted_output_cotangents, up)
    pulled = jnp.where(is_value[None, :], pulled[1], pulled[0])

    width = 2 * all_rows
    pieces = [
        jnp.concatenate([projected, pulled], axis=1)
        .astype(jnp.bfloat16)
        .reshape(ranks, -1, width)
    ] + [
        part[:, at : at + width].reshape(ranks, own_lines, width)
        for part in frozen_part
        for at in range(0, columns, width)
    ]
    sums = exchange(jnp.concatenate(pieces, axis=1), "tp").astype(jnp.float32).sum(axis=0)
    own_tokens = tokens // ranks
    frozen_sum = jnp.concatenate(
        [
            sums[at : at + own_lines]
            for at in range(own_tokens, sums.shape[0], own_lines)
        ],
        axis=1,
    )
    both = gather_over(sums[:own_tokens].astype(jnp.bfloat16), "tp", ranks).reshape(tokens, width)
    projected, pulled = both[:, :all_rows], both[:, all_rows:]

    down_gradient = ADAPTER_SCALE * product("tn,td->nd", pulled, trainer_token_inputs)
    up_gradient = product("jct,tn->jnc", weighted_output_cotangents, projected)
    up_gradient = ADAPTER_SCALE * jnp.where(is_value[:, None], up_gradient[1], up_gradient[0])

    totals = (
        exchange(
            side_by_side(down_gradient, up_gradient).reshape(groups, own_rows, -1), "grp"
        )
        .astype(jnp.float32)
        .sum(axis=0)
    )
    fresh_down = optimizer_update(
        own_down(adapter_down_master),
        totals[:, :own_width],
        own_down(down_first_moment),
        own_down(down_second_moment),
    )
    fresh_up = optimizer_update(
        own_up(adapter_up_master),
        totals[:, own_width : own_width + own_columns],
        own_up(up_first_moment),
        own_up(up_second_moment),
    )
    down, up = all_factors(fresh_down[0], fresh_up[0])
    adapter_part = product("rd,nd->rn", flat_inputs, down).reshape(ranks, own_lines, all_rows)

    up_copies = jnp.broadcast_to(up.transpose()[None], (ranks, own_columns, all_rows))
    last = exchange(jnp.concatenate([*two_terms(adapter_part), up_copies], axis=1), "tp")
    rank_space = last[:, : 2 * own_lines].astype(jnp.float32).sum(axis=0)
    rank_space = rank_space[:own_lines] + rank_space[own_lines:]
    full_up = last[:, 2 * own_lines :].reshape(columns, all_rows)
    adapter_sum = jnp.concatenate(
        [
            sum(
                product("rn,cn->rc", term, full_up)
                for term in two_terms(jnp.where(is_value[None, :] == bool(kind), rank_space, 0.0))
            )
            for kind in range(kinds)
        ],
        axis=1,
    )
    raw = frozen_sum + ADAPTER_SCALE * adapter_sum
    summed = raw.reshape(row_count, steps_count, kinds, columns)

    scaling = 1.0 / math.sqrt(head_size)
    query_heads = queries.reshape(row_count, steps_count, head_groups, -1, head_size)
    cache_scores = product("rtghe,rgpe->rtghp", query_heads, rotated_key_cache) * scaling
    valid = jnp.arange(cache_slots, dtype=jnp.int32)[None, :] < lengths[:, None]
    cache_scores = jnp.where(valid[:, None, None, None, :], cache_scores, MASKED)
    positions = lengths[:, None] + jnp.arange(steps_count, dtype=jnp.int32)[None, :]
    key_raw = summed[:, :, 0].reshape(row_count, steps_count, head_groups, head_size)
    new_keys = rotate_keys(key_raw, positions).reshape(
        row_count, steps_count, head_groups * head_size
    )
    new_values = summed[:, :, 1]
    key_entries = new_keys.astype(jnp.bfloat16)
    value_entries = new_values.astype(jnp.bfloat16)
    fresh_heads = key_entries.reshape(row_count, steps_count, head_groups, head_size)
    fresh_scores = (
        jnp.einsum(
            "rtghe,rsge->rtghs", query_heads, fresh_heads, preferred_element_type=jnp.float32
        )
        * scaling
    )
    causal = jnp.arange(steps_count)[:, None] >= jnp.arange(steps_count)[None, :]
    fresh_scores = jnp.where(causal[None, :, None, None, :], fresh_scores, MASKED)
    scores = jnp.concatenate([cache_scores, fresh_scores], axis=-1)
    peak_score = jnp.max(scores, axis=-1, keepdims=True)
    exponent = jnp.exp(scores - peak_score)
    weights = (exponent / jnp.sum(exponent, axis=-1, keepdims=True)).astype(jnp.bfloat16)
    fresh_value_heads = value_entries.reshape(row_count, steps_count, head_groups, head_size)
    result = jnp.einsum(
        "rtghp,rgpe->rtghe",
        weights[..., :cache_slots],
        stored_value_cache,
        preferred_element_type=jnp.float32,
    )
    result = result + jnp.einsum(
        "rtghs,rsge->rtghe",
        weights[..., cache_slots:],
        fresh_value_heads,
        preferred_element_type=jnp.float32,
    )
    attended = result.reshape(row_count, steps_count, query_width)

    def back_down(values):
        return values.reshape(kinds, own_rank, own_width)

    def back_up(values):
        return values.reshape(kinds, own_rank, own_columns).transpose(0, 2, 1)

    return (
        attended,
        new_keys,
        new_values,
        back_down(fresh_down[0]),
        back_up(fresh_up[0]),
        back_down(fresh_down[1]),
        back_down(fresh_down[2]),
        back_up(fresh_up[1]),
        back_up(fresh_up[2]),
    )


def solution(mesh):
    in_specs = (
        P("grp", "tp"),
        P(None, "tp", "grp"),
        P(None, "grp", "tp"),
        P(None, "tp", "grp"),
        P(None, "grp", "tp"),
        P(None, "grp", "tp"),
        P(None, "tp", "grp"),
        P(None, "tp", "grp"),
        P(None, "tp", None),
        P("grp", None, "tp"),
        P(("grp", "tp"), None, None),
        P(("grp", "tp"), None, None, None),
        P(("grp", "tp"), None, None, None),
        P(("grp", "tp")),
    )
    out_specs = (
        P(("grp", "tp"), None, None),
        P(("grp", "tp"), None, None),
        P(("grp", "tp"), None, None),
        P(None, "grp", "tp"),
        P(None, "tp", "grp"),
        P(None, "grp", "tp"),
        P(None, "grp", "tp"),
        P(None, "tp", "grp"),
        P(None, "tp", "grp"),
    )
    placed = functools.partial(body, mesh.shape["grp"], mesh.shape["tp"])
    return jax.shard_map(placed, mesh=mesh, in_specs=in_specs, out_specs=out_specs, check_vma=False)
```

```python
import functools
import math

import jax
import jax.numpy as jnp
from jax import lax
from jax.experimental import pallas as pl
from jax.experimental.pallas import tpu as pltpu
from jax.sharding import PartitionSpec as P

OPT_STEP = 20


ADAPTER_SCALE = 2.0
LEARN_RATE = 0.001
WEIGHT_DECAY = 0.01
BETA_FIRST = 0.9
BETA_SECOND = 0.95
EPSILON = 1e-08
THETA = 500000.0
ROPE_FACTOR = 8.0
LOW_FACTOR = 1.0
HIGH_FACTOR = 4.0
INITIAL_CONTEXT = 8192.0
MASKED = -1e30


def rope_frequencies(head_size):
    half_head = head_size // 2
    exponent = jnp.arange(half_head, dtype=jnp.float32) * (2.0 / head_size)
    base_frequency = jnp.power(jnp.float32(THETA), -exponent)
    wavelength = 2.0 * math.pi / base_frequency
    smooth = (INITIAL_CONTEXT / wavelength - LOW_FACTOR) / (HIGH_FACTOR - LOW_FACTOR)
    blended = (1.0 - smooth) * base_frequency / ROPE_FACTOR + smooth * base_frequency
    scaled = jnp.where(
        wavelength > INITIAL_CONTEXT / LOW_FACTOR, base_frequency / ROPE_FACTOR, blended
    )
    return jnp.where(wavelength < INITIAL_CONTEXT / HIGH_FACTOR, base_frequency, scaled)


def optimizer_update(current, gradient, moment_mean, moment_square):
    mean_next = BETA_FIRST * moment_mean + (1.0 - BETA_FIRST) * gradient
    square_next = BETA_SECOND * moment_square + (1.0 - BETA_SECOND) * gradient * gradient
    bias_first = 1.0 - BETA_FIRST**OPT_STEP
    bias_second = 1.0 - BETA_SECOND**OPT_STEP
    update = mean_next / bias_first / (jnp.sqrt(square_next / bias_second) + EPSILON)
    return (current - LEARN_RATE * (update + WEIGHT_DECAY * current), mean_next, square_next)


def exchange(pieces, axis):
    return lax.all_to_all(pieces, axis, 0, 0, tiled=True)


def gather_over(block, axis, count):
    return exchange(jnp.broadcast_to(block[None], (count,) + block.shape), axis)


def two_terms(values):
    high = lax.reduce_precision(values, 8, 7)
    return high.astype(jnp.bfloat16), (values - high).astype(jnp.bfloat16)


def product(spec, left, right):
    return jnp.einsum(spec, left, right, preferred_element_type=jnp.float32)


def scatter_sum_by_halves(values, axis, count):
    index = lax.axis_index(axis)
    bits = count.bit_length() - 1
    values = values.reshape((2,) * bits + values.shape[1:])
    left = list(range(bits - 1, -1, -1))
    for bit in [0] + list(range(bits - 1, 0, -1)):
        at = left.index(bit)
        left.remove(bit)
        low = lax.index_in_dim(values, 0, at, keepdims=False)
        high = lax.index_in_dim(values, 1, at, keepdims=False)
        upper = (index >> bit) & 1 == 1
        pairs = [(place, place ^ (1 << bit)) for place in range(count)]
        arrived = lax.ppermute(jnp.where(upper, low, high), axis, pairs)
        values = jnp.where(upper, high, low) + arrived
    return values


def dot_last(left, right):
    return lax.dot_general(
        left, right, (((1,), (1,)), ((), ())), preferred_element_type=jnp.float32
    )


def cached_attention(lengths_ref, query_ref, key_ref, value_ref, peak_ref, total_ref, sum_ref):
    row_count, heads, slots, size = key_ref.shape
    lines = query_ref.shape[1]
    steps = 4
    line = lax.broadcasted_iota(jnp.int32, (lines, slots), 0) // steps % row_count
    slot = lax.broadcasted_iota(jnp.int32, (lines, slots), 1)
    valid = [(line == row) & (slot < lengths_ref[row]) for row in range(row_count)]
    for head in range(heads):
        query = query_ref[head]
        scores = jnp.full((lines, slots), MASKED, jnp.float32)
        for row in range(row_count):
            found = dot_last(query, key_ref[row, head]) * (1.0 / math.sqrt(size))
            scores = jnp.where(valid[row], found, scores)
        peak = jnp.max(scores, axis=1, keepdims=True)
        weights = jnp.exp(scores - peak)
        result = jnp.zeros((lines, size), jnp.float32)
        for row in range(row_count):
            own = jnp.where(valid[row], weights, 0.0).astype(jnp.bfloat16)
            result += jnp.dot(own, value_ref[row, head], preferred_element_type=jnp.float32)
        peak_ref[head] = peak
        total_ref[head] = jnp.sum(weights, axis=1, keepdims=True)
        sum_ref[head] = result


def finish(
    last_ref,
    frozen_ref,
    cosine_ref,
    sine_ref,
    query_ref,
    peak_ref,
    total_ref,
    sum_ref,
    attended_ref,
    keys_ref,
    values_ref,
    own_rank,
):
    row_count, steps, _ = keys_ref.shape
    heads, lines, size = query_ref.shape
    own_lines = row_count * steps
    ranks, _, all_rows = last_ref.shape
    parts = jnp.sum(last_ref[:, : 2 * own_lines, :].astype(jnp.float32), axis=0)
    rank_space = parts[:own_lines] + parts[own_lines:]
    full_up = last_ref[:, 2 * own_lines :, :].reshape(-1, all_rows)
    columns = full_up.shape[0]
    adapter_row = lax.broadcasted_iota(jnp.int32, (own_lines, all_rows), 1)
    raw = []
    for kind in range(2):
        own = jnp.where(adapter_row // own_rank % 2 == kind, rank_space, 0.0)
        high = own.astype(jnp.bfloat16).astype(jnp.float32)
        both = jnp.concatenate([high, own - high], axis=0).astype(jnp.bfloat16)
        both = dot_last(both, full_up)
        raw.append(
            frozen_ref[:, kind * columns : (kind + 1) * columns]
            + ADAPTER_SCALE * (both[:own_lines] + both[own_lines:])
        )
    for row in range(row_count):
        values_ref[row] = raw[1][row * steps : (row + 1) * steps]

    line = lax.broadcasted_iota(jnp.int32, (lines, 2 * own_lines), 0)
    entry = lax.broadcasted_iota(jnp.int32, (lines, 2 * own_lines), 1)
    valid = (line // steps % row_count == entry // steps) & (entry % steps <= line % steps)
    for head in range(heads):
        lanes = slice(head * size, (head + 1) * size)
        vector = raw[0][:, lanes]
        turned = pltpu.roll(vector, size // 2, 1)
        rotated = vector * cosine_ref[...] + turned * sine_ref[...]
        for row in range(row_count):
            keys_ref[row, :, lanes] = rotated[row * steps : (row + 1) * steps]
        fresh_keys = jnp.concatenate([rotated, rotated], axis=0).astype(jnp.bfloat16)
        fresh_values = jnp.concatenate([raw[1][:, lanes]] * 2, axis=0).astype(jnp.bfloat16)
        scores = dot_last(query_ref[head], fresh_keys) * (1.0 / math.sqrt(size))
        scores = jnp.where(valid, scores, MASKED)
        peak = jnp.maximum(peak_ref[head], jnp.max(scores, axis=1, keepdims=True))
        scale = jnp.exp(peak_ref[head] - peak)
        weights = jnp.where(valid, jnp.exp(scores - peak), 0.0)
        total = total_ref[head] * scale + jnp.sum(weights, axis=1, keepdims=True)
        result = sum_ref[head] * scale + jnp.dot(
            weights.astype(jnp.bfloat16), fresh_values, preferred_element_type=jnp.float32
        )
        result = result * (1.0 / total)
        group = lines // own_lines
        for query_head in range(group):
            at = (head * group + query_head) * size
            for row in range(row_count):
                start = query_head * own_lines + row * steps
                attended_ref[row, :, at : at + size] = result[start : start + steps]


def body(
    groups,
    ranks,
    trainer_token_inputs,
    weighted_output_cotangents,
    adapter_down_master,
    adapter_up_master,
    down_first_moment,
    down_second_moment,
    up_first_moment,
    up_second_moment,
    frozen_weights,
    decode_step_inputs,
    queries,
    rotated_key_cache,
    stored_value_cache,
    lengths,
):
    row_count, steps_count, query_width = queries.shape
    head_groups, cache_slots, head_size = rotated_key_cache.shape[1:]
    kinds, own_rank, own_width = adapter_down_master.shape
    own_columns, tokens = weighted_output_cotangents.shape[1:]
    columns = own_columns * ranks
    own_rows = kinds * own_rank
    all_rows = own_rows * groups
    own_lines = row_count * steps_count
    lanes = 128
    fill = -own_columns % lanes
    is_value = (jnp.arange(all_rows) // own_rank) % kinds == 1

    def own_down(values):
        return values.reshape(own_rows, own_width)

    def own_up(values):
        return values.transpose(0, 2, 1).reshape(own_rows, own_columns)

    def side_by_side(down, up):
        parts = [down.astype(jnp.bfloat16), up.astype(jnp.bfloat16)]
        return jnp.concatenate([parts[0], jnp.pad(parts[1], ((0, 0), (0, fill)))], axis=1)

    def all_factors(down, up):
        both = gather_over(side_by_side(down, up), "grp", groups).reshape(all_rows, -1)
        return both[:, :own_width], both[:, own_width : own_width + own_columns]

    flat_inputs = decode_step_inputs.reshape(-1, own_width)
    frozen_part = [
        product("rd,dc->rc", flat_inputs, frozen_weights[kind]) for kind in range(kinds)
    ]
    frozen_sum = scatter_sum_by_halves(
        jnp.concatenate(frozen_part, axis=1).reshape(ranks, own_lines, kinds * columns),
        "tp",
        ranks,
    )

    down, up = all_factors(own_down(adapter_down_master), own_up(adapter_up_master))
    projected = product("td,nd->tn", trainer_token_inputs, down)
    pulled = product("jct,nc->jtn", weighted_output_cotangents, up)
    pulled = jnp.where(is_value[None, :], pulled[1], pulled[0])

    pieces = jnp.concatenate([projected, pulled], axis=1).astype(jnp.bfloat16)
    sums = (
        exchange(pieces.reshape(ranks, -1, 2 * all_rows), "tp").astype(jnp.float32).sum(axis=0)
    )
    both = gather_over(sums.astype(jnp.bfloat16), "tp", ranks).reshape(tokens, 2 * all_rows)
    projected, pulled = both[:, :all_rows], both[:, all_rows:]

    down_gradient = ADAPTER_SCALE * product("tn,td->nd", pulled, trainer_token_inputs)
    up_gradient = product("jct,tn->jnc", weighted_output_cotangents, projected)
    up_gradient = ADAPTER_SCALE * jnp.where(is_value[:, None], up_gradient[1], up_gradient[0])

    totals = (
        exchange(
            side_by_side(down_gradient, up_gradient).reshape(groups, own_rows, -1), "grp"
        )
        .astype(jnp.float32)
        .sum(axis=0)
    )
    fresh_down = optimizer_update(
        own_down(adapter_down_master),
        totals[:, :own_width],
        own_down(down_first_moment),
        own_down(down_second_moment),
    )
    fresh_up = optimizer_update(
        own_up(adapter_up_master),
        totals[:, own_width : own_width + own_columns],
        own_up(up_first_moment),
        own_up(up_second_moment),
    )
    down, up = all_factors(fresh_down[0], fresh_up[0])
    up, frozen_sum = lax.optimization_barrier((up, frozen_sum))
    adapter_part = product("rd,nd->rn", flat_inputs, down).reshape(ranks, own_lines, all_rows)

    up_copies = jnp.broadcast_to(up.transpose()[None], (ranks, own_columns, all_rows))
    last = exchange(jnp.concatenate([*two_terms(adapter_part), up_copies], axis=1), "tp")

    lines = query_width // (head_groups * head_size) * own_lines
    query_lines = (
        queries.reshape(row_count, steps_count, head_groups, -1, head_size)
        .transpose(2, 3, 0, 1, 4)
        .reshape(head_groups, lines, head_size)
    )
    column = jax.ShapeDtypeStruct((head_groups, lines, 1), jnp.float32)
    peak, total, cached = pl.pallas_call(
        cached_attention,
        out_shape=(
            column,
            column,
            jax.ShapeDtypeStruct((head_groups, lines, head_size), jnp.float32),
        ),
        in_specs=[pl.BlockSpec(memory_space=pltpu.SMEM)]
        + [pl.BlockSpec(memory_space=pltpu.VMEM)] * 3,
        cost_estimate=pl.CostEstimate(
            flops=8 * lines * cache_slots * head_size * head_groups,
            bytes_accessed=4 * row_count * head_groups * cache_slots * head_size,
            transcendentals=lines * cache_slots * head_groups,
        ),
    )(lengths, query_lines, rotated_key_cache, stored_value_cache)

    positions = lengths[:, None] + jnp.arange(steps_count, dtype=jnp.int32)[None, :]
    angles = positions.astype(jnp.float32).reshape(-1, 1) * rope_frequencies(head_size)
    cosine, sine = jnp.cos(angles), jnp.sin(angles)
    cosine = jnp.concatenate([cosine, cosine], axis=1)
    sine = jnp.concatenate([-sine, sine], axis=1)

    fresh = jax.ShapeDtypeStruct((row_count, steps_count, columns), jnp.float32)
    attended, new_keys, new_values = pl.pallas_call(
        functools.partial(finish, own_rank=own_rank),
        out_shape=(jax.ShapeDtypeStruct(queries.shape, jnp.float32), fresh, fresh),
        in_specs=[pl.BlockSpec(memory_space=pltpu.VMEM)] * 8,
        cost_estimate=pl.CostEstimate(
            flops=4 * lines * own_lines * head_size * head_groups,
            bytes_accessed=4 * queries.size,
            transcendentals=lines * own_lines * head_groups,
        ),
    )(last, frozen_sum, cosine, sine, query_lines, peak, total, cached)

    def back_down(values):
        return values.reshape(kinds, own_rank, own_width)

    def back_up(values):
        return values.reshape(kinds, own_rank, own_columns).transpose(0, 2, 1)

    return (
        attended,
        new_keys,
        new_values,
        back_down(fresh_down[0]),
        back_up(fresh_up[0]),
        back_down(fresh_down[1]),
        back_down(fresh_down[2]),
        back_up(fresh_up[1]),
        back_up(fresh_up[2]),
    )


def solution(mesh):
    in_specs = (
        P("grp", "tp"),
        P(None, "tp", "grp"),
        P(None, "grp", "tp"),
        P(None, "tp", "grp"),
        P(None, "grp", "tp"),
        P(None, "grp", "tp"),
        P(None, "tp", "grp"),
        P(None, "tp", "grp"),
        P(None, "tp", None),
        P("grp", None, "tp"),
        P(("grp", "tp"), None, None),
        P(("grp", "tp"), None, None, None),
        P(("grp", "tp"), None, None, None),
        P(("grp", "tp")),
    )
    out_specs = (
        P(("grp", "tp"), None, None),
        P(("grp", "tp"), None, None),
        P(("grp", "tp"), None, None),
        P(None, "grp", "tp"),
        P(None, "tp", "grp"),
        P(None, "grp", "tp"),
        P(None, "grp", "tp"),
        P(None, "tp", "grp"),
        P(None, "tp", "grp"),
    )
    placed = functools.partial(body, mesh.shape["grp"], mesh.shape["tp"])
    return jax.shard_map(placed, mesh=mesh, in_specs=in_specs, out_specs=out_specs, check_vma=False)
```

```python
import functools
import math

import jax
import jax.numpy as jnp
from jax import lax
from jax.experimental import pallas as pl
from jax.experimental.pallas import tpu as pltpu
from jax.sharding import PartitionSpec as P

OPT_STEP = 20


ADAPTER_SCALE = 2.0
LEARN_RATE = 0.001
WEIGHT_DECAY = 0.01
BETA_FIRST = 0.9
BETA_SECOND = 0.95
EPSILON = 1e-08
THETA = 500000.0
ROPE_FACTOR = 8.0
LOW_FACTOR = 1.0
HIGH_FACTOR = 4.0
INITIAL_CONTEXT = 8192.0
MASKED = -1e30
KERNEL_BYTES = 8 * 1024 * 1024


def rope_frequencies(head_size):
    half_head = head_size // 2
    exponent = jnp.arange(half_head, dtype=jnp.float32) * (2.0 / head_size)
    base_frequency = jnp.power(jnp.float32(THETA), -exponent)
    wavelength = 2.0 * math.pi / base_frequency
    smooth = (INITIAL_CONTEXT / wavelength - LOW_FACTOR) / (HIGH_FACTOR - LOW_FACTOR)
    blended = (1.0 - smooth) * base_frequency / ROPE_FACTOR + smooth * base_frequency
    scaled = jnp.where(
        wavelength > INITIAL_CONTEXT / LOW_FACTOR, base_frequency / ROPE_FACTOR, blended
    )
    return jnp.where(wavelength < INITIAL_CONTEXT / HIGH_FACTOR, base_frequency, scaled)


def optimizer_update(current, gradient, moment_mean, moment_square):
    mean_next = BETA_FIRST * moment_mean + (1.0 - BETA_FIRST) * gradient
    square_next = BETA_SECOND * moment_square + (1.0 - BETA_SECOND) * gradient * gradient
    bias_first = 1.0 - BETA_FIRST**OPT_STEP
    bias_second = 1.0 - BETA_SECOND**OPT_STEP
    update = mean_next / bias_first / (jnp.sqrt(square_next / bias_second) + EPSILON)
    return (current - LEARN_RATE * (update + WEIGHT_DECAY * current), mean_next, square_next)


def exchange(pieces, axis):
    return lax.all_to_all(pieces, axis, 0, 0, tiled=True)


def product(spec, left, right):
    return jnp.einsum(spec, left, right, preferred_element_type=jnp.float32)


def scatter_sum_by_halves(values, axis, count, before_last):
    index = lax.axis_index(axis)
    bits = count.bit_length() - 1
    values = values.reshape((2,) * bits + values.shape[1:])
    left = list(range(bits - 1, -1, -1))
    for bit in [0] + list(range(bits - 1, 0, -1)):
        if len(left) == 1:
            before_last, values = lax.optimization_barrier((before_last, values))
        at = left.index(bit)
        left.remove(bit)
        low = lax.index_in_dim(values, 0, at, keepdims=False)
        high = lax.index_in_dim(values, 1, at, keepdims=False)
        upper = (index >> bit) & 1 == 1
        pairs = [(place, place ^ (1 << bit)) for place in range(count)]
        arrived = lax.ppermute(jnp.where(upper, low, high), axis, pairs)
        values = jnp.where(upper, high, low) + arrived
    return before_last, values


def dot_last(left, right):
    return lax.dot_general(
        left, right, (((1,), (1,)), ((), ())), preferred_element_type=jnp.float32
    )


def dot_first(left, right):
    return lax.dot_general(
        left, right, (((0,), (0,)), ((), ())), preferred_element_type=jnp.float32
    )


def kind_of_row(shape, own_rank):
    return lax.broadcasted_iota(jnp.int32, shape, 0) // own_rank % 2


def stack_kinds(ref):
    return jnp.concatenate([ref[0], ref[1]], axis=0)


def send_masters(down_ref, up_ref, out_ref):
    groups, _, wide = out_ref.shape
    own_rank, own_width = down_ref.shape[1:]
    own_columns = up_ref.shape[2]
    rest = wide - own_width
    rows = []
    for kind in range(2):
        line = up_ref[kind]
        before = jnp.zeros((own_rank, kind * own_columns), jnp.float32)
        after = jnp.zeros((own_rank, rest - (kind + 1) * own_columns), jnp.float32)
        parts = [part for part in (before, line, after) if part.shape[1]]
        rows.append(jnp.concatenate(parts, axis=1))
    block = jnp.concatenate([stack_kinds(down_ref), jnp.concatenate(rows, axis=0)], axis=1)
    block = block.astype(jnp.bfloat16)
    for group in range(groups):
        out_ref[group] = block


def project_tokens(factors_ref, inputs_ref, cotangents_ref, out_ref):
    all_rows = factors_ref.shape[0]
    own_width = inputs_ref.shape[1]
    both = cotangents_ref.shape[0]
    projected = dot_last(inputs_ref[...], factors_ref[:, :own_width])
    pulled = lax.dot_general(
        cotangents_ref[...],
        factors_ref[:, own_width : own_width + both],
        (((0,), (1,)), ((), ())),
        preferred_element_type=jnp.float32,
    )
    out_ref[:, :all_rows] = projected.astype(jnp.bfloat16)
    out_ref[:, all_rows:] = pulled.astype(jnp.bfloat16)


def sum_tokens(parts_ref, out_ref):
    total = jnp.sum(parts_ref[...].astype(jnp.float32), axis=0).astype(jnp.bfloat16)
    for rank in range(out_ref.shape[0]):
        out_ref[rank] = total


def send_gradients(tokens_ref, inputs_ref, cotangents_ref, out_ref, own_rank):
    groups, own_rows, wide = out_ref.shape
    all_rows = groups * own_rows
    own_width = inputs_ref.shape[1]
    both = cotangents_ref.shape[0]
    down = ADAPTER_SCALE * dot_first(tokens_ref[:, all_rows:], inputs_ref[...])
    cotangents = cotangents_ref[...]
    if wide - own_width > both:
        empty = jnp.zeros((wide - own_width - both, cotangents.shape[1]), jnp.bfloat16)
        cotangents = jnp.concatenate([cotangents, empty], axis=0)
    up = lax.dot_general(
        tokens_ref[:, :all_rows],
        cotangents,
        (((0,), (1,)), ((), ())),
        preferred_element_type=jnp.float32,
    )
    lane_kind = lax.broadcasted_iota(jnp.int32, up.shape, 1) // (both // 2)
    up = jnp.where(lane_kind == kind_of_row(up.shape, own_rank), ADAPTER_SCALE * up, 0.0)
    down = down.astype(jnp.bfloat16)
    up = up.astype(jnp.bfloat16)
    for group in range(groups):
        rows = slice(group * own_rows, (group + 1) * own_rows)
        out_ref[group, :, :own_width] = down[rows]
        out_ref[group, :, own_width:] = up[rows]


def update_factors(
    parts_ref,
    down_ref,
    down_first_ref,
    down_second_ref,
    up_ref,
    up_first_ref,
    up_second_ref,
    fresh_down_ref,
    fresh_down_first_ref,
    fresh_down_second_ref,
    fresh_up_ref,
    fresh_up_first_ref,
    fresh_up_second_ref,
    out_ref,
):
    groups = out_ref.shape[0]
    own_rank, own_width = down_ref.shape[1:]
    gradient = jnp.sum(parts_ref[...].astype(jnp.float32), axis=0)
    down = optimizer_update(
        stack_kinds(down_ref),
        gradient[:, :own_width],
        stack_kinds(down_first_ref),
        stack_kinds(down_second_ref),
    )
    up = optimizer_update(
        up_ref[...], gradient[:, own_width:], up_first_ref[...], up_second_ref[...]
    )
    for ref, values in zip(
        (fresh_down_ref, fresh_down_first_ref, fresh_down_second_ref), down
    ):
        for kind in range(2):
            ref[kind] = values[kind * own_rank : (kind + 1) * own_rank]
    for ref, values in zip((fresh_up_ref, fresh_up_first_ref, fresh_up_second_ref), up):
        ref[...] = values
    block = jnp.concatenate([down[0], up[0]], axis=1).astype(jnp.bfloat16)
    for group in range(groups):
        out_ref[group] = block


def send_rank_space(factors_ref, inputs_ref, out_ref, own_lines):
    ranks, height, _ = out_ref.shape
    own_columns = height - 2 * own_lines
    own_width = inputs_ref.shape[1]
    values = dot_last(inputs_ref[...], factors_ref[:, :own_width])
    high = values.astype(jnp.bfloat16).astype(jnp.float32)
    low = values - high
    up = factors_ref[:, own_width:].astype(jnp.float32).T
    up = (up[:own_columns] + up[own_columns : 2 * own_columns]).astype(jnp.bfloat16)
    for rank in range(ranks):
        rows = slice(rank * own_lines, (rank + 1) * own_lines)
        both = jnp.concatenate([high[rows], low[rows]], axis=0)
        out_ref[rank, : 2 * own_lines] = both.astype(jnp.bfloat16)
        out_ref[rank, 2 * own_lines :] = up


def cached_attention(lengths_ref, query_ref, key_ref, value_ref, peak_ref, total_ref, sum_ref):
    row_count, heads, slots, size = key_ref.shape
    lines = query_ref.shape[1]
    steps = 4
    line = lax.broadcasted_iota(jnp.int32, (lines, slots), 0) // steps % row_count
    slot = lax.broadcasted_iota(jnp.int32, (lines, slots), 1)
    valid = [(line == row) & (slot < lengths_ref[row]) for row in range(row_count)]
    for head in range(heads):
        query = query_ref[head]
        scores = jnp.full((lines, slots), MASKED, jnp.float32)
        for row in range(row_count):
            found = dot_last(query, key_ref[row, head]) * (1.0 / math.sqrt(size))
            scores = jnp.where(valid[row], found, scores)
        peak = jnp.max(scores, axis=1, keepdims=True)
        weights = jnp.exp(scores - peak)
        result = jnp.zeros((lines, size), jnp.float32)
        for row in range(row_count):
            own = jnp.where(valid[row], weights, 0.0).astype(jnp.bfloat16)
            result += jnp.dot(own, value_ref[row, head], preferred_element_type=jnp.float32)
        peak_ref[head] = peak
        total_ref[head] = jnp.sum(weights, axis=1, keepdims=True)
        sum_ref[head] = result


def finish(
    last_ref,
    frozen_ref,
    cosine_ref,
    sine_ref,
    query_ref,
    peak_ref,
    total_ref,
    sum_ref,
    attended_ref,
    keys_ref,
    values_ref,
    own_rank,
):
    row_count, steps, _ = keys_ref.shape
    heads, lines, size = query_ref.shape
    own_lines = row_count * steps
    ranks, _, all_rows = last_ref.shape
    parts = jnp.sum(last_ref[:, : 2 * own_lines, :].astype(jnp.float32), axis=0)
    rank_space = parts[:own_lines] + parts[own_lines:]
    full_up = last_ref[:, 2 * own_lines :, :].reshape(-1, all_rows)
    columns = full_up.shape[0]
    adapter_row = lax.broadcasted_iota(jnp.int32, (own_lines, all_rows), 1)
    raw = []
    for kind in range(2):
        own = jnp.where(adapter_row // own_rank % 2 == kind, rank_space, 0.0)
        high = own.astype(jnp.bfloat16).astype(jnp.float32)
        both = jnp.concatenate([high, own - high], axis=0).astype(jnp.bfloat16)
        both = dot_last(both, full_up)
        raw.append(
            frozen_ref[:, kind * columns : (kind + 1) * columns]
            + ADAPTER_SCALE * (both[:own_lines] + both[own_lines:])
        )
    for row in range(row_count):
        values_ref[row] = raw[1][row * steps : (row + 1) * steps]

    line = lax.broadcasted_iota(jnp.int32, (lines, 2 * own_lines), 0)
    entry = lax.broadcasted_iota(jnp.int32, (lines, 2 * own_lines), 1)
    valid = (line // steps % row_count == entry // steps) & (entry % steps <= line % steps)
    for head in range(heads):
        lanes = slice(head * size, (head + 1) * size)
        vector = raw[0][:, lanes]
        turned = pltpu.roll(vector, size // 2, 1)
        rotated = vector * cosine_ref[...] + turned * sine_ref[...]
        for row in range(row_count):
            keys_ref[row, :, lanes] = rotated[row * steps : (row + 1) * steps]
        fresh_keys = jnp.concatenate([rotated, rotated], axis=0).astype(jnp.bfloat16)
        fresh_values = jnp.concatenate([raw[1][:, lanes]] * 2, axis=0).astype(jnp.bfloat16)
        scores = dot_last(query_ref[head], fresh_keys) * (1.0 / math.sqrt(size))
        scores = jnp.where(valid, scores, MASKED)
        peak = jnp.maximum(peak_ref[head], jnp.max(scores, axis=1, keepdims=True))
        scale = jnp.exp(peak_ref[head] - peak)
        weights = jnp.where(valid, jnp.exp(scores - peak), 0.0)
        total = total_ref[head] * scale + jnp.sum(weights, axis=1, keepdims=True)
        result = sum_ref[head] * scale + jnp.dot(
            weights.astype(jnp.bfloat16), fresh_values, preferred_element_type=jnp.float32
        )
        result = result * (1.0 / total)
        group = lines // own_lines
        for query_head in range(group):
            at = (head * group + query_head) * size
            for row in range(row_count):
                start = query_head * own_lines + row * steps
                attended_ref[row, :, at : at + size] = result[start : start + steps]


def body(
    groups,
    ranks,
    trainer_token_inputs,
    weighted_output_cotangents,
    adapter_down_master,
    adapter_up_master,
    down_first_moment,
    down_second_moment,
    up_first_moment,
    up_second_moment,
    frozen_weights,
    decode_step_inputs,
    queries,
    rotated_key_cache,
    stored_value_cache,
    lengths,
):
    row_count, steps_count, query_width = queries.shape
    head_groups, cache_slots, head_size = rotated_key_cache.shape[1:]
    kinds, own_rank, own_width = adapter_down_master.shape
    own_columns, tokens = weighted_output_cotangents.shape[1:]
    columns = own_columns * ranks
    own_rows = kinds * own_rank
    all_rows = own_rows * groups
    own_lines = row_count * steps_count
    wide = own_width + -(-kinds * own_columns // 128) * 128

    def by_rank(values):
        return values.transpose(0, 2, 1)

    def placed(values):
        rest = wide - own_width - own_columns
        return jnp.concatenate(
            [
                jnp.pad(by_rank(values)[kind], ((0, 0), (at, rest - at)))
                for kind, at in ((0, 0), (1, own_columns))
            ]
        )

    def brought_back(values):
        blocks = [
            values[kind * own_rank : (kind + 1) * own_rank, at : at + own_columns]
            for kind, at in ((0, 0), (1, own_columns))
        ]
        return by_rank(jnp.stack(blocks))

    def call(kernel, outs, *operands):
        flops = 4 * max(operand.size for operand in operands)
        return pl.pallas_call(
            kernel,
            out_shape=outs,
            in_specs=[pl.BlockSpec(memory_space=pltpu.VMEM)] * len(operands),
            compiler_params=pltpu.CompilerParams(vmem_limit_bytes=KERNEL_BYTES),
            cost_estimate=pl.CostEstimate(
                flops=flops, bytes_accessed=flops, transcendentals=0
            ),
        )(*operands)

    def out(shape, kind=jnp.bfloat16):
        return jax.ShapeDtypeStruct(shape, kind)

    flat_inputs = decode_step_inputs.reshape(-1, own_width)
    frozen_part = jnp.concatenate(
        [product("rd,dc->rc", flat_inputs, frozen_weights[kind]) for kind in range(kinds)], axis=1
    ).reshape(ranks, own_lines, kinds * columns)

    sent = out((groups, own_rows, wide))
    masters = call(send_masters, sent, adapter_down_master, by_rank(adapter_up_master))
    factors = exchange(masters, "grp").reshape(all_rows, wide)

    cotangents = weighted_output_cotangents.reshape(-1, tokens)
    shares = call(
        project_tokens, out((tokens, 2 * all_rows)), factors, trainer_token_inputs, cotangents
    ).reshape(ranks, -1, 2 * all_rows)
    sums = call(sum_tokens, out(shares.shape), exchange(shares, "tp"))
    token_sums = exchange(sums, "tp").reshape(tokens, 2 * all_rows)

    gradients = call(
        functools.partial(send_gradients, own_rank=own_rank),
        sent,
        token_sums,
        trainer_token_inputs,
        cotangents,
    )
    gradients, frozen_sum = scatter_sum_by_halves(frozen_part, "tp", ranks, gradients)
    own = out(adapter_down_master.shape, jnp.float32)
    small = out((own_rows, wide - own_width), jnp.float32)
    *fresh, fresh_factors = call(
        update_factors,
        (own, own, own, small, small, small, sent),
        exchange(gradients, "grp"),
        adapter_down_master,
        down_first_moment,
        down_second_moment,
        placed(adapter_up_master),
        placed(up_first_moment),
        placed(up_second_moment),
    )
    fresh_factors, frozen_sum = lax.optimization_barrier((fresh_factors, frozen_sum))
    factors = exchange(fresh_factors, "grp").reshape(all_rows, wide)

    rank_space = call(
        functools.partial(send_rank_space, own_lines=own_lines),
        out((ranks, 2 * own_lines + own_columns, all_rows)),
        factors,
        flat_inputs,
    )

    lines = query_width // (head_groups * head_size) * own_lines
    query_lines = (
        queries.reshape(row_count, steps_count, head_groups, -1, head_size)
        .transpose(2, 3, 0, 1, 4)
        .reshape(head_groups, lines, head_size)
    )
    column = jax.ShapeDtypeStruct((head_groups, lines, 1), jnp.float32)
    peak, total, cached = pl.pallas_call(
        cached_attention,
        out_shape=(
            column,
            column,
            jax.ShapeDtypeStruct((head_groups, lines, head_size), jnp.float32),
        ),
        in_specs=[pl.BlockSpec(memory_space=pltpu.SMEM)]
        + [pl.BlockSpec(memory_space=pltpu.VMEM)] * 3,
        compiler_params=pltpu.CompilerParams(vmem_limit_bytes=KERNEL_BYTES),
        cost_estimate=pl.CostEstimate(
            flops=8 * lines * cache_slots * head_size * head_groups,
            bytes_accessed=4 * row_count * head_groups * cache_slots * head_size,
            transcendentals=lines * cache_slots * head_groups,
        ),
    )(lengths, query_lines, rotated_key_cache, stored_value_cache)

    positions = lengths[:, None] + jnp.arange(steps_count, dtype=jnp.int32)[None, :]
    angles = positions.astype(jnp.float32).reshape(-1, 1) * rope_frequencies(head_size)
    cosine, sine = jnp.cos(angles), jnp.sin(angles)
    cosine = jnp.concatenate([cosine, cosine], axis=1)
    sine = jnp.concatenate([-sine, sine], axis=1)

    rank_space, peak, total, cached, cosine, sine = lax.optimization_barrier(
        (rank_space, peak, total, cached, cosine, sine)
    )
    last = exchange(rank_space, "tp")
    entries = jax.ShapeDtypeStruct((row_count, steps_count, columns), jnp.float32)
    attended, new_keys, new_values = pl.pallas_call(
        functools.partial(finish, own_rank=own_rank),
        out_shape=(jax.ShapeDtypeStruct(queries.shape, jnp.float32), entries, entries),
        in_specs=[pl.BlockSpec(memory_space=pltpu.VMEM)] * 8,
        compiler_params=pltpu.CompilerParams(vmem_limit_bytes=KERNEL_BYTES),
        cost_estimate=pl.CostEstimate(
            flops=4 * lines * own_lines * head_size * head_groups,
            bytes_accessed=4 * queries.size,
            transcendentals=lines * own_lines * head_groups,
        ),
    )(last, frozen_sum, cosine, sine, query_lines, peak, total, cached)

    return (
        attended,
        new_keys,
        new_values,
        fresh[0],
        brought_back(fresh[3]),
        fresh[1],
        fresh[2],
        brought_back(fresh[4]),
        brought_back(fresh[5]),
    )


def solution(mesh):
    in_specs = (
        P("grp", "tp"),
        P(None, "tp", "grp"),
        P(None, "grp", "tp"),
        P(None, "tp", "grp"),
        P(None, "grp", "tp"),
        P(None, "grp", "tp"),
        P(None, "tp", "grp"),
        P(None, "tp", "grp"),
        P(None, "tp", None),
        P("grp", None, "tp"),
        P(("grp", "tp"), None, None),
        P(("grp", "tp"), None, None, None),
        P(("grp", "tp"), None, None, None),
        P(("grp", "tp")),
    )
    out_specs = (
        P(("grp", "tp"), None, None),
        P(("grp", "tp"), None, None),
        P(("grp", "tp"), None, None),
        P(None, "grp", "tp"),
        P(None, "tp", "grp"),
        P(None, "grp", "tp"),
        P(None, "grp", "tp"),
        P(None, "tp", "grp"),
        P(None, "tp", "grp"),
    )
    placed = functools.partial(body, mesh.shape["grp"], mesh.shape["tp"])
    return jax.shard_map(placed, mesh=mesh, in_specs=in_specs, out_specs=out_specs, check_vma=False)
```

```python
import functools
import math

import jax
import jax.numpy as jnp
from jax import lax
from jax.experimental import pallas as pl
from jax.experimental.pallas import tpu as pltpu
from jax.sharding import PartitionSpec as P

OPT_STEP = 20


ADAPTER_SCALE = 2.0
LEARN_RATE = 0.001
WEIGHT_DECAY = 0.01
BETA_FIRST = 0.9
BETA_SECOND = 0.95
EPSILON = 1e-08
THETA = 500000.0
ROPE_FACTOR = 8.0
LOW_FACTOR = 1.0
HIGH_FACTOR = 4.0
INITIAL_CONTEXT = 8192.0
MASKED = -1e30
KERNEL_BYTES = 8 * 1024 * 1024


def rope_frequencies(head_size):
    half_head = head_size // 2
    exponent = jnp.arange(half_head, dtype=jnp.float32) * (2.0 / head_size)
    base_frequency = jnp.power(jnp.float32(THETA), -exponent)
    wavelength = 2.0 * math.pi / base_frequency
    smooth = (INITIAL_CONTEXT / wavelength - LOW_FACTOR) / (HIGH_FACTOR - LOW_FACTOR)
    blended = (1.0 - smooth) * base_frequency / ROPE_FACTOR + smooth * base_frequency
    scaled = jnp.where(
        wavelength > INITIAL_CONTEXT / LOW_FACTOR, base_frequency / ROPE_FACTOR, blended
    )
    return jnp.where(wavelength < INITIAL_CONTEXT / HIGH_FACTOR, base_frequency, scaled)


def optimizer_update(current, gradient, moment_mean, moment_square):
    mean_next = BETA_FIRST * moment_mean + (1.0 - BETA_FIRST) * gradient
    square_next = BETA_SECOND * moment_square + (1.0 - BETA_SECOND) * gradient * gradient
    bias_first = 1.0 - BETA_FIRST**OPT_STEP
    bias_second = 1.0 - BETA_SECOND**OPT_STEP
    update = mean_next / bias_first / (jnp.sqrt(square_next / bias_second) + EPSILON)
    return (current - LEARN_RATE * (update + WEIGHT_DECAY * current), mean_next, square_next)


def exchange(pieces, axis):
    return lax.all_to_all(pieces, axis, 0, 0, tiled=True)


def product(spec, left, right):
    return jnp.einsum(spec, left, right, preferred_element_type=jnp.float32)


def scatter_sum_by_halves(values, axis, count):
    index = lax.axis_index(axis)
    bits = count.bit_length() - 1
    values = values.reshape((2,) * bits + values.shape[1:])
    left = list(range(bits - 1, -1, -1))
    for bit in [0] + list(range(bits - 1, 0, -1)):
        at = left.index(bit)
        left.remove(bit)
        low = lax.index_in_dim(values, 0, at, keepdims=False)
        high = lax.index_in_dim(values, 1, at, keepdims=False)
        upper = (index >> bit) & 1 == 1
        pairs = [(place, place ^ (1 << bit)) for place in range(count)]
        arrived = lax.ppermute(jnp.where(upper, low, high), axis, pairs)
        values = jnp.where(upper, high, low) + arrived
    return values


def dot_last(left, right):
    return lax.dot_general(
        left, right, (((1,), (1,)), ((), ())), preferred_element_type=jnp.float32
    )


def dot_first(left, right):
    return lax.dot_general(
        left, right, (((0,), (0,)), ((), ())), preferred_element_type=jnp.float32
    )


def kind_of_row(shape, own_rank):
    return lax.broadcasted_iota(jnp.int32, shape, 0) // own_rank % 2


def stack_kinds(ref):
    return jnp.concatenate([ref[0], ref[1]], axis=0)


def send_masters(down_ref, up_ref, out_ref):
    groups, _, wide = out_ref.shape
    own_rank, own_width = down_ref.shape[1:]
    own_columns = up_ref.shape[2]
    rest = wide - own_width
    rows = []
    for kind in range(2):
        line = up_ref[kind]
        before = jnp.zeros((own_rank, kind * own_columns), jnp.float32)
        after = jnp.zeros((own_rank, rest - (kind + 1) * own_columns), jnp.float32)
        parts = [part for part in (before, line, after) if part.shape[1]]
        rows.append(jnp.concatenate(parts, axis=1))
    block = jnp.concatenate([stack_kinds(down_ref), jnp.concatenate(rows, axis=0)], axis=1)
    block = block.astype(jnp.bfloat16)
    for group in range(groups):
        out_ref[group] = block


def project_tokens(factors_ref, inputs_ref, cotangents_ref, out_ref):
    all_rows = factors_ref.shape[0]
    own_width = inputs_ref.shape[1]
    both = cotangents_ref.shape[0]
    projected = dot_last(inputs_ref[...], factors_ref[:, :own_width])
    pulled = lax.dot_general(
        cotangents_ref[...],
        factors_ref[:, own_width : own_width + both],
        (((0,), (1,)), ((), ())),
        preferred_element_type=jnp.float32,
    )
    out_ref[:, :all_rows] = projected.astype(jnp.bfloat16)
    out_ref[:, all_rows:] = pulled.astype(jnp.bfloat16)


def sum_tokens(parts_ref, out_ref):
    total = jnp.sum(parts_ref[...].astype(jnp.float32), axis=0).astype(jnp.bfloat16)
    for rank in range(out_ref.shape[0]):
        out_ref[rank] = total


def send_gradients(tokens_ref, inputs_ref, cotangents_ref, out_ref, own_rank):
    groups, own_rows, wide = out_ref.shape
    all_rows = groups * own_rows
    own_width = inputs_ref.shape[1]
    both = cotangents_ref.shape[0]
    down = ADAPTER_SCALE * dot_first(tokens_ref[:, all_rows:], inputs_ref[...])
    cotangents = cotangents_ref[...]
    if wide - own_width > both:
        empty = jnp.zeros((wide - own_width - both, cotangents.shape[1]), jnp.bfloat16)
        cotangents = jnp.concatenate([cotangents, empty], axis=0)
    up = lax.dot_general(
        tokens_ref[:, :all_rows],
        cotangents,
        (((0,), (1,)), ((), ())),
        preferred_element_type=jnp.float32,
    )
    lane_kind = lax.broadcasted_iota(jnp.int32, up.shape, 1) // (both // 2)
    up = jnp.where(lane_kind == kind_of_row(up.shape, own_rank), ADAPTER_SCALE * up, 0.0)
    down = down.astype(jnp.bfloat16)
    up = up.astype(jnp.bfloat16)
    for group in range(groups):
        rows = slice(group * own_rows, (group + 1) * own_rows)
        out_ref[group, :, :own_width] = down[rows]
        out_ref[group, :, own_width:] = up[rows]


def update_factors(
    parts_ref,
    down_ref,
    down_first_ref,
    down_second_ref,
    up_ref,
    up_first_ref,
    up_second_ref,
    fresh_down_ref,
    fresh_down_first_ref,
    fresh_down_second_ref,
    fresh_up_ref,
    fresh_up_first_ref,
    fresh_up_second_ref,
    out_ref,
):
    groups = out_ref.shape[0]
    own_rank, own_width = down_ref.shape[1:]
    gradient = jnp.sum(parts_ref[...].astype(jnp.float32), axis=0)
    down = optimizer_update(
        stack_kinds(down_ref),
        gradient[:, :own_width],
        stack_kinds(down_first_ref),
        stack_kinds(down_second_ref),
    )
    up = optimizer_update(
        up_ref[...], gradient[:, own_width:], up_first_ref[...], up_second_ref[...]
    )
    for ref, values in zip(
        (fresh_down_ref, fresh_down_first_ref, fresh_down_second_ref), down
    ):
        for kind in range(2):
            ref[kind] = values[kind * own_rank : (kind + 1) * own_rank]
    for ref, values in zip((fresh_up_ref, fresh_up_first_ref, fresh_up_second_ref), up):
        ref[...] = values
    block = jnp.concatenate([down[0], up[0]], axis=1).astype(jnp.bfloat16)
    for group in range(groups):
        out_ref[group] = block


def send_rank_space(factors_ref, inputs_ref, out_ref, own_lines):
    ranks, height, _ = out_ref.shape
    own_columns = height - 2 * own_lines
    own_width = inputs_ref.shape[1]
    values = dot_last(inputs_ref[...], factors_ref[:, :own_width])
    high = values.astype(jnp.bfloat16).astype(jnp.float32)
    low = values - high
    up = factors_ref[:, own_width:].astype(jnp.float32).T
    up = (up[:own_columns] + up[own_columns : 2 * own_columns]).astype(jnp.bfloat16)
    for rank in range(ranks):
        rows = slice(rank * own_lines, (rank + 1) * own_lines)
        both = jnp.concatenate([high[rows], low[rows]], axis=0)
        out_ref[rank, : 2 * own_lines] = both.astype(jnp.bfloat16)
        out_ref[rank, 2 * own_lines :] = up


def cached_attention(lengths_ref, query_ref, key_ref, value_ref, peak_ref, total_ref, sum_ref):
    row_count, heads, slots, size = key_ref.shape
    lines = query_ref.shape[1]
    steps = 4
    line = lax.broadcasted_iota(jnp.int32, (lines, slots), 0) // steps % row_count
    slot = lax.broadcasted_iota(jnp.int32, (lines, slots), 1)
    valid = [(line == row) & (slot < lengths_ref[row]) for row in range(row_count)]
    for head in range(heads):
        query = query_ref[head]
        scores = jnp.full((lines, slots), MASKED, jnp.float32)
        for row in range(row_count):
            found = dot_last(query, key_ref[row, head]) * (1.0 / math.sqrt(size))
            scores = jnp.where(valid[row], found, scores)
        peak = jnp.max(scores, axis=1, keepdims=True)
        weights = jnp.exp(scores - peak)
        result = jnp.zeros((lines, size), jnp.float32)
        for row in range(row_count):
            own = jnp.where(valid[row], weights, 0.0).astype(jnp.bfloat16)
            result += jnp.dot(own, value_ref[row, head], preferred_element_type=jnp.float32)
        peak_ref[head] = peak
        total_ref[head] = jnp.sum(weights, axis=1, keepdims=True)
        sum_ref[head] = result


def finish(
    last_ref,
    frozen_ref,
    cosine_ref,
    sine_ref,
    query_ref,
    peak_ref,
    total_ref,
    sum_ref,
    attended_ref,
    keys_ref,
    values_ref,
    own_rank,
):
    row_count, steps, _ = keys_ref.shape
    heads, lines, size = query_ref.shape
    own_lines = row_count * steps
    ranks, _, all_rows = last_ref.shape
    parts = jnp.sum(last_ref[:, : 2 * own_lines, :].astype(jnp.float32), axis=0)
    rank_space = parts[:own_lines] + parts[own_lines:]
    full_up = last_ref[:, 2 * own_lines :, :].reshape(-1, all_rows)
    columns = full_up.shape[0]
    adapter_row = lax.broadcasted_iota(jnp.int32, (own_lines, all_rows), 1)
    raw = []
    for kind in range(2):
        own = jnp.where(adapter_row // own_rank % 2 == kind, rank_space, 0.0)
        high = own.astype(jnp.bfloat16).astype(jnp.float32)
        both = jnp.concatenate([high, own - high], axis=0).astype(jnp.bfloat16)
        both = dot_last(both, full_up)
        raw.append(
            frozen_ref[:, kind * columns : (kind + 1) * columns]
            + ADAPTER_SCALE * (both[:own_lines] + both[own_lines:])
        )
    for row in range(row_count):
        values_ref[row] = raw[1][row * steps : (row + 1) * steps]

    line = lax.broadcasted_iota(jnp.int32, (lines, 2 * own_lines), 0)
    entry = lax.broadcasted_iota(jnp.int32, (lines, 2 * own_lines), 1)
    valid = (line // steps % row_count == entry // steps) & (entry % steps <= line % steps)
    for head in range(heads):
        lanes = slice(head * size, (head + 1) * size)
        vector = raw[0][:, lanes]
        turned = pltpu.roll(vector, size // 2, 1)
        rotated = vector * cosine_ref[...] + turned * sine_ref[...]
        for row in range(row_count):
            keys_ref[row, :, lanes] = rotated[row * steps : (row + 1) * steps]
        fresh_keys = jnp.concatenate([rotated, rotated], axis=0).astype(jnp.bfloat16)
        fresh_values = jnp.concatenate([raw[1][:, lanes]] * 2, axis=0).astype(jnp.bfloat16)
        scores = dot_last(query_ref[head], fresh_keys) * (1.0 / math.sqrt(size))
        scores = jnp.where(valid, scores, MASKED)
        peak = jnp.maximum(peak_ref[head], jnp.max(scores, axis=1, keepdims=True))
        scale = jnp.exp(peak_ref[head] - peak)
        weights = jnp.where(valid, jnp.exp(scores - peak), 0.0)
        total = total_ref[head] * scale + jnp.sum(weights, axis=1, keepdims=True)
        result = sum_ref[head] * scale + jnp.dot(
            weights.astype(jnp.bfloat16), fresh_values, preferred_element_type=jnp.float32
        )
        result = result * (1.0 / total)
        group = lines // own_lines
        for query_head in range(group):
            at = (head * group + query_head) * size
            for row in range(row_count):
                start = query_head * own_lines + row * steps
                attended_ref[row, :, at : at + size] = result[start : start + steps]


def body(
    groups,
    ranks,
    trainer_token_inputs,
    weighted_output_cotangents,
    adapter_down_master,
    adapter_up_master,
    down_first_moment,
    down_second_moment,
    up_first_moment,
    up_second_moment,
    frozen_weights,
    decode_step_inputs,
    queries,
    rotated_key_cache,
    stored_value_cache,
    lengths,
):
    row_count, steps_count, query_width = queries.shape
    head_groups, cache_slots, head_size = rotated_key_cache.shape[1:]
    kinds, own_rank, own_width = adapter_down_master.shape
    own_columns, tokens = weighted_output_cotangents.shape[1:]
    columns = own_columns * ranks
    own_rows = kinds * own_rank
    all_rows = own_rows * groups
    own_lines = row_count * steps_count
    wide = own_width + -(-kinds * own_columns // 128) * 128

    def by_rank(values):
        return values.transpose(0, 2, 1)

    def placed(values):
        rest = wide - own_width - own_columns
        return jnp.concatenate(
            [
                jnp.pad(by_rank(values)[kind], ((0, 0), (at, rest - at)))
                for kind, at in ((0, 0), (1, own_columns))
            ]
        )

    def brought_back(values):
        blocks = [
            values[kind * own_rank : (kind + 1) * own_rank, at : at + own_columns]
            for kind, at in ((0, 0), (1, own_columns))
        ]
        return by_rank(jnp.stack(blocks))

    def call(kernel, outs, *operands):
        flops = 4 * max(operand.size for operand in operands)
        return pl.pallas_call(
            kernel,
            out_shape=outs,
            in_specs=[pl.BlockSpec(memory_space=pltpu.VMEM)] * len(operands),
            compiler_params=pltpu.CompilerParams(vmem_limit_bytes=KERNEL_BYTES),
            cost_estimate=pl.CostEstimate(
                flops=flops, bytes_accessed=flops, transcendentals=0
            ),
        )(*operands)

    def out(shape, kind=jnp.bfloat16):
        return jax.ShapeDtypeStruct(shape, kind)

    flat_inputs = decode_step_inputs.reshape(-1, own_width)
    frozen_part = jnp.concatenate(
        [product("rd,dc->rc", flat_inputs, frozen_weights[kind]) for kind in range(kinds)], axis=1
    ).reshape(ranks, own_lines, kinds * columns)
    frozen_sum = scatter_sum_by_halves(frozen_part, "tp", ranks)

    lines = query_width // (head_groups * head_size) * own_lines
    query_lines = (
        queries.reshape(row_count, steps_count, head_groups, -1, head_size)
        .transpose(2, 3, 0, 1, 4)
        .reshape(head_groups, lines, head_size)
    )
    column = jax.ShapeDtypeStruct((head_groups, lines, 1), jnp.float32)
    peak, total, cached = pl.pallas_call(
        cached_attention,
        out_shape=(
            column,
            column,
            jax.ShapeDtypeStruct((head_groups, lines, head_size), jnp.float32),
        ),
        in_specs=[pl.BlockSpec(memory_space=pltpu.SMEM)]
        + [pl.BlockSpec(memory_space=pltpu.VMEM)] * 3,
        compiler_params=pltpu.CompilerParams(vmem_limit_bytes=KERNEL_BYTES),
        cost_estimate=pl.CostEstimate(
            flops=8 * lines * cache_slots * head_size * head_groups,
            bytes_accessed=4 * row_count * head_groups * cache_slots * head_size,
            transcendentals=lines * cache_slots * head_groups,
        ),
    )(lengths, query_lines, rotated_key_cache, stored_value_cache)

    sent = out((groups, own_rows, wide))
    masters = call(send_masters, sent, adapter_down_master, by_rank(adapter_up_master))
    factors = exchange(masters, "grp").reshape(all_rows, wide)

    cotangents = weighted_output_cotangents.reshape(-1, tokens)
    shares = call(
        project_tokens, out((tokens, 2 * all_rows)), factors, trainer_token_inputs, cotangents
    ).reshape(ranks, -1, 2 * all_rows)
    sums = call(sum_tokens, out(shares.shape), exchange(shares, "tp"))
    token_sums = exchange(sums, "tp").reshape(tokens, 2 * all_rows)

    gradients = call(
        functools.partial(send_gradients, own_rank=own_rank),
        sent,
        token_sums,
        trainer_token_inputs,
        cotangents,
    )
    gradients, peak, total, cached = lax.optimization_barrier((gradients, peak, total, cached))
    own = out(adapter_down_master.shape, jnp.float32)
    small = out((own_rows, wide - own_width), jnp.float32)
    *fresh, fresh_factors = call(
        update_factors,
        (own, own, own, small, small, small, sent),
        exchange(gradients, "grp"),
        adapter_down_master,
        down_first_moment,
        down_second_moment,
        placed(adapter_up_master),
        placed(up_first_moment),
        placed(up_second_moment),
    )
    factors = exchange(fresh_factors, "grp").reshape(all_rows, wide)

    rank_space = call(
        functools.partial(send_rank_space, own_lines=own_lines),
        out((ranks, 2 * own_lines + own_columns, all_rows)),
        factors,
        flat_inputs,
    )

    positions = lengths[:, None] + jnp.arange(steps_count, dtype=jnp.int32)[None, :]
    angles = positions.astype(jnp.float32).reshape(-1, 1) * rope_frequencies(head_size)
    cosine, sine = jnp.cos(angles), jnp.sin(angles)
    cosine = jnp.concatenate([cosine, cosine], axis=1)
    sine = jnp.concatenate([-sine, sine], axis=1)

    rank_space, frozen_sum = lax.optimization_barrier((rank_space, frozen_sum))
    last = exchange(rank_space, "tp")
    entries = jax.ShapeDtypeStruct((row_count, steps_count, columns), jnp.float32)
    attended, new_keys, new_values = pl.pallas_call(
        functools.partial(finish, own_rank=own_rank),
        out_shape=(jax.ShapeDtypeStruct(queries.shape, jnp.float32), entries, entries),
        in_specs=[pl.BlockSpec(memory_space=pltpu.VMEM)] * 8,
        compiler_params=pltpu.CompilerParams(vmem_limit_bytes=KERNEL_BYTES),
        cost_estimate=pl.CostEstimate(
            flops=4 * lines * own_lines * head_size * head_groups,
            bytes_accessed=4 * queries.size,
            transcendentals=lines * own_lines * head_groups,
        ),
    )(last, frozen_sum, cosine, sine, query_lines, peak, total, cached)

    return (
        attended,
        new_keys,
        new_values,
        fresh[0],
        brought_back(fresh[3]),
        fresh[1],
        fresh[2],
        brought_back(fresh[4]),
        brought_back(fresh[5]),
    )


def solution(mesh):
    in_specs = (
        P("grp", "tp"),
        P(None, "tp", "grp"),
        P(None, "grp", "tp"),
        P(None, "tp", "grp"),
        P(None, "grp", "tp"),
        P(None, "grp", "tp"),
        P(None, "tp", "grp"),
        P(None, "tp", "grp"),
        P(None, "tp", None),
        P("grp", None, "tp"),
        P(("grp", "tp"), None, None),
        P(("grp", "tp"), None, None, None),
        P(("grp", "tp"), None, None, None),
        P(("grp", "tp")),
    )
    out_specs = (
        P(("grp", "tp"), None, None),
        P(("grp", "tp"), None, None),
        P(("grp", "tp"), None, None),
        P(None, "grp", "tp"),
        P(None, "tp", "grp"),
        P(None, "grp", "tp"),
        P(None, "grp", "tp"),
        P(None, "tp", "grp"),
        P(None, "tp", "grp"),
    )
    placed = functools.partial(body, mesh.shape["grp"], mesh.shape["tp"])
    return jax.shard_map(placed, mesh=mesh, in_specs=in_specs, out_specs=out_specs, check_vma=False)
```

```python
import functools
import math

import jax
import jax.numpy as jnp
from jax import lax
from jax.experimental import pallas as pl
from jax.experimental.pallas import tpu as pltpu
from jax.sharding import PartitionSpec as P

OPT_STEP = 20


ADAPTER_SCALE = 2.0
LEARN_RATE = 0.001
WEIGHT_DECAY = 0.01
BETA_FIRST = 0.9
BETA_SECOND = 0.95
EPSILON = 1e-08
THETA = 500000.0
ROPE_FACTOR = 8.0
LOW_FACTOR = 1.0
HIGH_FACTOR = 4.0
INITIAL_CONTEXT = 8192.0
MASKED = -1e30
KERNEL_BYTES = 8 * 1024 * 1024


def rope_frequencies(head_size):
    half_head = head_size // 2
    exponent = jnp.arange(half_head, dtype=jnp.float32) * (2.0 / head_size)
    base_frequency = jnp.power(jnp.float32(THETA), -exponent)
    wavelength = 2.0 * math.pi / base_frequency
    smooth = (INITIAL_CONTEXT / wavelength - LOW_FACTOR) / (HIGH_FACTOR - LOW_FACTOR)
    blended = (1.0 - smooth) * base_frequency / ROPE_FACTOR + smooth * base_frequency
    scaled = jnp.where(
        wavelength > INITIAL_CONTEXT / LOW_FACTOR, base_frequency / ROPE_FACTOR, blended
    )
    return jnp.where(wavelength < INITIAL_CONTEXT / HIGH_FACTOR, base_frequency, scaled)


def optimizer_update(current, gradient, moment_mean, moment_square):
    mean_next = BETA_FIRST * moment_mean + (1.0 - BETA_FIRST) * gradient
    square_next = BETA_SECOND * moment_square + (1.0 - BETA_SECOND) * gradient * gradient
    bias_first = 1.0 - BETA_FIRST**OPT_STEP
    bias_second = 1.0 - BETA_SECOND**OPT_STEP
    update = mean_next / bias_first / (jnp.sqrt(square_next / bias_second) + EPSILON)
    return (current - LEARN_RATE * (update + WEIGHT_DECAY * current), mean_next, square_next)


def exchange(pieces, axis):
    return lax.all_to_all(pieces, axis, 0, 0, tiled=True)


def product(spec, left, right):
    return jnp.einsum(spec, left, right, preferred_element_type=jnp.float32)


def after(values, earlier):
    return lax.optimization_barrier((values, earlier))[0]


def half_sum(values, axis, count, at, bit, earlier_sum=None, earlier_send=None):
    if earlier_send is not None:
        values = after(values, earlier_send)
    low = lax.index_in_dim(values, 0, at, keepdims=False)
    high = lax.index_in_dim(values, 1, at, keepdims=False)
    upper = (lax.axis_index(axis) >> bit) & 1 == 1
    pairs = [(place, place ^ (1 << bit)) for place in range(count)]
    arrived = lax.ppermute(jnp.where(upper, low, high), axis, pairs)
    kept = jnp.where(upper, high, low)
    if earlier_sum is not None:
        kept = after(kept, earlier_sum)
    return kept + arrived


def dot_last(left, right):
    return lax.dot_general(
        left, right, (((1,), (1,)), ((), ())), preferred_element_type=jnp.float32
    )


def dot_first(left, right):
    return lax.dot_general(
        left, right, (((0,), (0,)), ((), ())), preferred_element_type=jnp.float32
    )


def kind_of_row(shape, own_rank):
    return lax.broadcasted_iota(jnp.int32, shape, 0) // own_rank % 2


def stack_kinds(ref):
    return jnp.concatenate([ref[0], ref[1]], axis=0)


def send_masters(down_ref, up_ref, out_ref):
    groups, _, wide = out_ref.shape
    own_rank, own_width = down_ref.shape[1:]
    own_columns = up_ref.shape[2]
    rest = wide - own_width
    rows = []
    for kind in range(2):
        line = up_ref[kind]
        before = jnp.zeros((own_rank, kind * own_columns), jnp.float32)
        after = jnp.zeros((own_rank, rest - (kind + 1) * own_columns), jnp.float32)
        parts = [part for part in (before, line, after) if part.shape[1]]
        rows.append(jnp.concatenate(parts, axis=1))
    block = jnp.concatenate([stack_kinds(down_ref), jnp.concatenate(rows, axis=0)], axis=1)
    block = block.astype(jnp.bfloat16)
    for group in range(groups):
        out_ref[group] = block


def project_tokens(factors_ref, inputs_ref, cotangents_ref, out_ref):
    all_rows = factors_ref.shape[0]
    own_width = inputs_ref.shape[1]
    both = cotangents_ref.shape[0]
    projected = dot_last(inputs_ref[...], factors_ref[:, :own_width])
    pulled = lax.dot_general(
        cotangents_ref[...],
        factors_ref[:, own_width : own_width + both],
        (((0,), (1,)), ((), ())),
        preferred_element_type=jnp.float32,
    )
    out_ref[:, :all_rows] = projected.astype(jnp.bfloat16)
    out_ref[:, all_rows:] = pulled.astype(jnp.bfloat16)


def sum_tokens(parts_ref, out_ref):
    total = jnp.sum(parts_ref[...].astype(jnp.float32), axis=0).astype(jnp.bfloat16)
    for rank in range(out_ref.shape[0]):
        out_ref[rank] = total


def send_gradients(tokens_ref, inputs_ref, cotangents_ref, out_ref, own_rank):
    groups, own_rows, wide = out_ref.shape
    all_rows = groups * own_rows
    own_width = inputs_ref.shape[1]
    both = cotangents_ref.shape[0]
    down = ADAPTER_SCALE * dot_first(tokens_ref[:, all_rows:], inputs_ref[...])
    cotangents = cotangents_ref[...]
    if wide - own_width > both:
        empty = jnp.zeros((wide - own_width - both, cotangents.shape[1]), jnp.bfloat16)
        cotangents = jnp.concatenate([cotangents, empty], axis=0)
    up = lax.dot_general(
        tokens_ref[:, :all_rows],
        cotangents,
        (((0,), (1,)), ((), ())),
        preferred_element_type=jnp.float32,
    )
    lane_kind = lax.broadcasted_iota(jnp.int32, up.shape, 1) // (both // 2)
    up = jnp.where(lane_kind == kind_of_row(up.shape, own_rank), ADAPTER_SCALE * up, 0.0)
    down = down.astype(jnp.bfloat16)
    up = up.astype(jnp.bfloat16)
    for group in range(groups):
        rows = slice(group * own_rows, (group + 1) * own_rows)
        out_ref[group, :, :own_width] = down[rows]
        out_ref[group, :, own_width:] = up[rows]


def update_factors(
    parts_ref,
    down_ref,
    down_first_ref,
    down_second_ref,
    up_ref,
    up_first_ref,
    up_second_ref,
    fresh_down_ref,
    fresh_down_first_ref,
    fresh_down_second_ref,
    fresh_up_ref,
    fresh_up_first_ref,
    fresh_up_second_ref,
    out_ref,
):
    groups = out_ref.shape[0]
    own_rank, own_width = down_ref.shape[1:]
    gradient = jnp.sum(parts_ref[...].astype(jnp.float32), axis=0)
    down = optimizer_update(
        stack_kinds(down_ref),
        gradient[:, :own_width],
        stack_kinds(down_first_ref),
        stack_kinds(down_second_ref),
    )
    up = optimizer_update(
        up_ref[...], gradient[:, own_width:], up_first_ref[...], up_second_ref[...]
    )
    for ref, values in zip(
        (fresh_down_ref, fresh_down_first_ref, fresh_down_second_ref), down
    ):
        for kind in range(2):
            ref[kind] = values[kind * own_rank : (kind + 1) * own_rank]
    for ref, values in zip((fresh_up_ref, fresh_up_first_ref, fresh_up_second_ref), up):
        ref[...] = values
    block = jnp.concatenate([down[0], up[0]], axis=1).astype(jnp.bfloat16)
    for group in range(groups):
        out_ref[group] = block


def send_rank_space(factors_ref, inputs_ref, out_ref, own_lines):
    ranks, height, _ = out_ref.shape
    own_columns = height - 2 * own_lines
    own_width = inputs_ref.shape[1]
    values = dot_last(inputs_ref[...], factors_ref[:, :own_width])
    high = values.astype(jnp.bfloat16).astype(jnp.float32)
    low = values - high
    up = factors_ref[:, own_width:].astype(jnp.float32).T
    up = (up[:own_columns] + up[own_columns : 2 * own_columns]).astype(jnp.bfloat16)
    for rank in range(ranks):
        rows = slice(rank * own_lines, (rank + 1) * own_lines)
        both = jnp.concatenate([high[rows], low[rows]], axis=0)
        out_ref[rank, : 2 * own_lines] = both.astype(jnp.bfloat16)
        out_ref[rank, 2 * own_lines :] = up


def cached_attention(lengths_ref, query_ref, key_ref, value_ref, peak_ref, total_ref, sum_ref):
    row_count, heads, slots, size = key_ref.shape
    lines = query_ref.shape[1]
    steps = 4
    line = lax.broadcasted_iota(jnp.int32, (lines, slots), 0) // steps % row_count
    slot = lax.broadcasted_iota(jnp.int32, (lines, slots), 1)
    valid = [(line == row) & (slot < lengths_ref[row]) for row in range(row_count)]
    for head in range(heads):
        query = query_ref[head]
        scores = jnp.full((lines, slots), MASKED, jnp.float32)
        for row in range(row_count):
            found = dot_last(query, key_ref[row, head]) * (1.0 / math.sqrt(size))
            scores = jnp.where(valid[row], found, scores)
        peak = jnp.max(scores, axis=1, keepdims=True)
        weights = jnp.exp(scores - peak)
        result = jnp.zeros((lines, size), jnp.float32)
        for row in range(row_count):
            own = jnp.where(valid[row], weights, 0.0).astype(jnp.bfloat16)
            result += jnp.dot(own, value_ref[row, head], preferred_element_type=jnp.float32)
        peak_ref[head] = peak
        total_ref[head] = jnp.sum(weights, axis=1, keepdims=True)
        sum_ref[head] = result


def finish(
    last_ref,
    frozen_ref,
    cosine_ref,
    sine_ref,
    query_ref,
    peak_ref,
    total_ref,
    sum_ref,
    attended_ref,
    keys_ref,
    values_ref,
    own_rank,
):
    row_count, steps, _ = keys_ref.shape
    heads, lines, size = query_ref.shape
    own_lines = row_count * steps
    ranks, _, all_rows = last_ref.shape
    parts = jnp.sum(last_ref[:, : 2 * own_lines, :].astype(jnp.float32), axis=0)
    rank_space = parts[:own_lines] + parts[own_lines:]
    full_up = last_ref[:, 2 * own_lines :, :].reshape(-1, all_rows)
    columns = full_up.shape[0]
    adapter_row = lax.broadcasted_iota(jnp.int32, (own_lines, all_rows), 1)
    raw = []
    for kind in range(2):
        own = jnp.where(adapter_row // own_rank % 2 == kind, rank_space, 0.0)
        high = own.astype(jnp.bfloat16).astype(jnp.float32)
        both = jnp.concatenate([high, own - high], axis=0).astype(jnp.bfloat16)
        both = dot_last(both, full_up)
        raw.append(
            frozen_ref[:, kind * columns : (kind + 1) * columns]
            + ADAPTER_SCALE * (both[:own_lines] + both[own_lines:])
        )
    for row in range(row_count):
        values_ref[row] = raw[1][row * steps : (row + 1) * steps]

    line = lax.broadcasted_iota(jnp.int32, (lines, 2 * own_lines), 0)
    entry = lax.broadcasted_iota(jnp.int32, (lines, 2 * own_lines), 1)
    valid = (line // steps % row_count == entry // steps) & (entry % steps <= line % steps)
    for head in range(heads):
        lanes = slice(head * size, (head + 1) * size)
        vector = raw[0][:, lanes]
        turned = pltpu.roll(vector, size // 2, 1)
        rotated = vector * cosine_ref[...] + turned * sine_ref[...]
        for row in range(row_count):
            keys_ref[row, :, lanes] = rotated[row * steps : (row + 1) * steps]
        fresh_keys = jnp.concatenate([rotated, rotated], axis=0).astype(jnp.bfloat16)
        fresh_values = jnp.concatenate([raw[1][:, lanes]] * 2, axis=0).astype(jnp.bfloat16)
        scores = dot_last(query_ref[head], fresh_keys) * (1.0 / math.sqrt(size))
        scores = jnp.where(valid, scores, MASKED)
        peak = jnp.maximum(peak_ref[head], jnp.max(scores, axis=1, keepdims=True))
        scale = jnp.exp(peak_ref[head] - peak)
        weights = jnp.where(valid, jnp.exp(scores - peak), 0.0)
        total = total_ref[head] * scale + jnp.sum(weights, axis=1, keepdims=True)
        result = sum_ref[head] * scale + jnp.dot(
            weights.astype(jnp.bfloat16), fresh_values, preferred_element_type=jnp.float32
        )
        result = result * (1.0 / total)
        group = lines // own_lines
        for query_head in range(group):
            at = (head * group + query_head) * size
            for row in range(row_count):
                start = query_head * own_lines + row * steps
                attended_ref[row, :, at : at + size] = result[start : start + steps]


def body(
    groups,
    ranks,
    trainer_token_inputs,
    weighted_output_cotangents,
    adapter_down_master,
    adapter_up_master,
    down_first_moment,
    down_second_moment,
    up_first_moment,
    up_second_moment,
    frozen_weights,
    decode_step_inputs,
    queries,
    rotated_key_cache,
    stored_value_cache,
    lengths,
):
    row_count, steps_count, query_width = queries.shape
    head_groups, cache_slots, head_size = rotated_key_cache.shape[1:]
    kinds, own_rank, own_width = adapter_down_master.shape
    own_columns, tokens = weighted_output_cotangents.shape[1:]
    columns = own_columns * ranks
    own_rows = kinds * own_rank
    all_rows = own_rows * groups
    own_lines = row_count * steps_count
    wide = own_width + -(-kinds * own_columns // 128) * 128

    def by_rank(values):
        return values.transpose(0, 2, 1)

    def placed(values):
        rest = wide - own_width - own_columns
        return jnp.concatenate(
            [
                jnp.pad(by_rank(values)[kind], ((0, 0), (at, rest - at)))
                for kind, at in ((0, 0), (1, own_columns))
            ]
        )

    def brought_back(values):
        blocks = [
            values[kind * own_rank : (kind + 1) * own_rank, at : at + own_columns]
            for kind, at in ((0, 0), (1, own_columns))
        ]
        return by_rank(jnp.stack(blocks))

    def call(kernel, outs, *operands):
        flops = 4 * max(operand.size for operand in operands)
        return pl.pallas_call(
            kernel,
            out_shape=outs,
            in_specs=[pl.BlockSpec(memory_space=pltpu.VMEM)] * len(operands),
            compiler_params=pltpu.CompilerParams(vmem_limit_bytes=KERNEL_BYTES),
            cost_estimate=pl.CostEstimate(
                flops=flops, bytes_accessed=flops, transcendentals=0
            ),
        )(*operands)

    def out(shape, kind=jnp.bfloat16):
        return jax.ShapeDtypeStruct(shape, kind)

    flat_inputs = decode_step_inputs.reshape(-1, own_width)

    lines = query_width // (head_groups * head_size) * own_lines
    query_lines = (
        queries.reshape(row_count, steps_count, head_groups, -1, head_size)
        .transpose(2, 3, 0, 1, 4)
        .reshape(head_groups, lines, head_size)
    )
    column = jax.ShapeDtypeStruct((head_groups, lines, 1), jnp.float32)
    peak, total, cached = pl.pallas_call(
        cached_attention,
        out_shape=(
            column,
            column,
            jax.ShapeDtypeStruct((head_groups, lines, head_size), jnp.float32),
        ),
        in_specs=[pl.BlockSpec(memory_space=pltpu.SMEM)]
        + [pl.BlockSpec(memory_space=pltpu.VMEM)] * 3,
        compiler_params=pltpu.CompilerParams(vmem_limit_bytes=KERNEL_BYTES),
        cost_estimate=pl.CostEstimate(
            flops=8 * lines * cache_slots * head_size * head_groups,
            bytes_accessed=4 * row_count * head_groups * cache_slots * head_size,
            transcendentals=lines * cache_slots * head_groups,
        ),
    )(lengths, query_lines, rotated_key_cache, stored_value_cache)

    sent = out((groups, own_rows, wide))
    masters = call(send_masters, sent, adapter_down_master, by_rank(adapter_up_master))
    later_inputs = after(flat_inputs, masters)
    frozen_part = jnp.concatenate(
        [product("rd,dc->rc", later_inputs, frozen_weights[kind]) for kind in range(kinds)], axis=1
    ).reshape(ranks, own_lines, kinds * columns)
    bits = ranks.bit_length() - 1
    frozen_part = frozen_part.reshape((2,) * bits + (own_lines, kinds * columns))
    factors = exchange(masters, "grp").reshape(all_rows, wide)

    frozen_part = half_sum(frozen_part, "tp", ranks, bits - 1, 0, earlier_sum=factors)
    frozen_part = half_sum(frozen_part, "tp", ranks, 0, bits - 1)

    cotangents = weighted_output_cotangents.reshape(-1, tokens)
    shares = call(
        project_tokens, out((tokens, 2 * all_rows)), factors, trainer_token_inputs, cotangents
    ).reshape(ranks, -1, 2 * all_rows)
    sums = call(sum_tokens, out(shares.shape), exchange(shares, "tp"))
    token_sums = exchange(sums, "tp").reshape(tokens, 2 * all_rows)

    gradients = call(
        functools.partial(send_gradients, own_rank=own_rank),
        sent,
        token_sums,
        trainer_token_inputs,
        cotangents,
    )
    frozen_part = half_sum(frozen_part, "tp", ranks, 0, 2, earlier_send=gradients)
    gradients, peak, total, cached = lax.optimization_barrier((gradients, peak, total, cached))
    own = out(adapter_down_master.shape, jnp.float32)
    small = out((own_rows, wide - own_width), jnp.float32)
    *fresh, fresh_factors = call(
        update_factors,
        (own, own, own, small, small, small, sent),
        exchange(gradients, "grp"),
        adapter_down_master,
        down_first_moment,
        down_second_moment,
        placed(adapter_up_master),
        placed(up_first_moment),
        placed(up_second_moment),
    )
    frozen_sum = half_sum(frozen_part, "tp", ranks, 0, 1, earlier_send=fresh_factors)
    factors = exchange(fresh_factors, "grp").reshape(all_rows, wide)

    rank_space = call(
        functools.partial(send_rank_space, own_lines=own_lines),
        out((ranks, 2 * own_lines + own_columns, all_rows)),
        factors,
        flat_inputs,
    )

    positions = lengths[:, None] + jnp.arange(steps_count, dtype=jnp.int32)[None, :]
    angles = positions.astype(jnp.float32).reshape(-1, 1) * rope_frequencies(head_size)
    cosine, sine = jnp.cos(angles), jnp.sin(angles)
    cosine = jnp.concatenate([cosine, cosine], axis=1)
    sine = jnp.concatenate([-sine, sine], axis=1)

    rank_space, frozen_sum = lax.optimization_barrier((rank_space, frozen_sum))
    last = exchange(rank_space, "tp")
    entries = jax.ShapeDtypeStruct((row_count, steps_count, columns), jnp.float32)
    attended, new_keys, new_values = pl.pallas_call(
        functools.partial(finish, own_rank=own_rank),
        out_shape=(jax.ShapeDtypeStruct(queries.shape, jnp.float32), entries, entries),
        in_specs=[pl.BlockSpec(memory_space=pltpu.VMEM)] * 8,
        compiler_params=pltpu.CompilerParams(vmem_limit_bytes=KERNEL_BYTES),
        cost_estimate=pl.CostEstimate(
            flops=4 * lines * own_lines * head_size * head_groups,
            bytes_accessed=4 * queries.size,
            transcendentals=lines * own_lines * head_groups,
        ),
    )(last, frozen_sum, cosine, sine, query_lines, peak, total, cached)

    return (
        attended,
        new_keys,
        new_values,
        fresh[0],
        brought_back(fresh[3]),
        fresh[1],
        fresh[2],
        brought_back(fresh[4]),
        brought_back(fresh[5]),
    )


def solution(mesh):
    in_specs = (
        P("grp", "tp"),
        P(None, "tp", "grp"),
        P(None, "grp", "tp"),
        P(None, "tp", "grp"),
        P(None, "grp", "tp"),
        P(None, "grp", "tp"),
        P(None, "tp", "grp"),
        P(None, "tp", "grp"),
        P(None, "tp", None),
        P("grp", None, "tp"),
        P(("grp", "tp"), None, None),
        P(("grp", "tp"), None, None, None),
        P(("grp", "tp"), None, None, None),
        P(("grp", "tp")),
    )
    out_specs = (
        P(("grp", "tp"), None, None),
        P(("grp", "tp"), None, None),
        P(("grp", "tp"), None, None),
        P(None, "grp", "tp"),
        P(None, "tp", "grp"),
        P(None, "grp", "tp"),
        P(None, "grp", "tp"),
        P(None, "tp", "grp"),
        P(None, "tp", "grp"),
    )
    placed = functools.partial(body, mesh.shape["grp"], mesh.shape["tp"])
    return jax.shard_map(placed, mesh=mesh, in_specs=in_specs, out_specs=out_specs, check_vma=False)
```

```python
import functools
import math

import jax
import jax.numpy as jnp
from jax import lax
from jax.experimental import pallas as pl
from jax.experimental.pallas import tpu as pltpu
from jax.sharding import PartitionSpec as P

OPT_STEP = 20


ADAPTER_SCALE = 2.0
LEARN_RATE = 0.001
WEIGHT_DECAY = 0.01
BETA_FIRST = 0.9
BETA_SECOND = 0.95
EPSILON = 1e-08
THETA = 500000.0
ROPE_FACTOR = 8.0
LOW_FACTOR = 1.0
HIGH_FACTOR = 4.0
INITIAL_CONTEXT = 8192.0
MASKED = -1e30
KERNEL_BYTES = 8 * 1024 * 1024


def rope_frequencies(head_size):
    half_head = head_size // 2
    exponent = jnp.arange(half_head, dtype=jnp.float32) * (2.0 / head_size)
    base_frequency = jnp.power(jnp.float32(THETA), -exponent)
    wavelength = 2.0 * math.pi / base_frequency
    smooth = (INITIAL_CONTEXT / wavelength - LOW_FACTOR) / (HIGH_FACTOR - LOW_FACTOR)
    blended = (1.0 - smooth) * base_frequency / ROPE_FACTOR + smooth * base_frequency
    scaled = jnp.where(
        wavelength > INITIAL_CONTEXT / LOW_FACTOR, base_frequency / ROPE_FACTOR, blended
    )
    return jnp.where(wavelength < INITIAL_CONTEXT / HIGH_FACTOR, base_frequency, scaled)


def optimizer_update(current, gradient, moment_mean, moment_square):
    mean_next = BETA_FIRST * moment_mean + (1.0 - BETA_FIRST) * gradient
    square_next = BETA_SECOND * moment_square + (1.0 - BETA_SECOND) * gradient * gradient
    bias_first = 1.0 - BETA_FIRST**OPT_STEP
    bias_second = 1.0 - BETA_SECOND**OPT_STEP
    update = mean_next / bias_first / (jnp.sqrt(square_next / bias_second) + EPSILON)
    return (current - LEARN_RATE * (update + WEIGHT_DECAY * current), mean_next, square_next)


def exchange(pieces, axis):
    return lax.all_to_all(pieces, axis, 0, 0, tiled=True)


def product(spec, left, right):
    return jnp.einsum(spec, left, right, preferred_element_type=jnp.float32)


def after(values, earlier):
    return lax.optimization_barrier((values, earlier))[0]


def half_sum(values, axis, count, at, bit, earlier_sum=None, earlier_send=None):
    if earlier_send is not None:
        values = after(values, earlier_send)
    low = lax.index_in_dim(values, 0, at, keepdims=False)
    high = lax.index_in_dim(values, 1, at, keepdims=False)
    upper = (lax.axis_index(axis) >> bit) & 1 == 1
    pairs = [(place, place ^ (1 << bit)) for place in range(count)]
    arrived = lax.ppermute(jnp.where(upper, low, high), axis, pairs)
    kept = jnp.where(upper, high, low)
    if earlier_sum is not None:
        kept = after(kept, earlier_sum)
    return kept + arrived


def dot_last(left, right):
    return lax.dot_general(
        left, right, (((1,), (1,)), ((), ())), preferred_element_type=jnp.float32
    )


def dot_first(left, right):
    return lax.dot_general(
        left, right, (((0,), (0,)), ((), ())), preferred_element_type=jnp.float32
    )


def kind_of_row(shape, own_rank):
    return lax.broadcasted_iota(jnp.int32, shape, 0) // own_rank % 2


def stack_kinds(ref):
    return jnp.concatenate([ref[0], ref[1]], axis=0)


def send_masters(down_ref, up_ref, out_ref):
    groups, _, wide = out_ref.shape
    own_rank, own_width = down_ref.shape[1:]
    own_columns = up_ref.shape[2]
    rest = wide - own_width
    rows = []
    for kind in range(2):
        line = up_ref[kind]
        before = jnp.zeros((own_rank, kind * own_columns), jnp.float32)
        after = jnp.zeros((own_rank, rest - (kind + 1) * own_columns), jnp.float32)
        parts = [part for part in (before, line, after) if part.shape[1]]
        rows.append(jnp.concatenate(parts, axis=1))
    block = jnp.concatenate([stack_kinds(down_ref), jnp.concatenate(rows, axis=0)], axis=1)
    block = block.astype(jnp.bfloat16)
    for group in range(groups):
        out_ref[group] = block


def project_tokens(factors_ref, inputs_ref, cotangents_ref, out_ref):
    all_rows = factors_ref.shape[0]
    own_width = inputs_ref.shape[1]
    both = cotangents_ref.shape[0]
    projected = dot_last(inputs_ref[...], factors_ref[:, :own_width])
    pulled = lax.dot_general(
        cotangents_ref[...],
        factors_ref[:, own_width : own_width + both],
        (((0,), (1,)), ((), ())),
        preferred_element_type=jnp.float32,
    )
    out_ref[:, :all_rows] = projected.astype(jnp.bfloat16)
    out_ref[:, all_rows:] = pulled.astype(jnp.bfloat16)


def sum_tokens(parts_ref, out_ref):
    total = jnp.sum(parts_ref[...].astype(jnp.float32), axis=0).astype(jnp.bfloat16)
    for rank in range(out_ref.shape[0]):
        out_ref[rank] = total


def send_gradients(tokens_ref, inputs_ref, cotangents_ref, out_ref, own_rank):
    groups, own_rows, wide = out_ref.shape
    all_rows = groups * own_rows
    own_width = inputs_ref.shape[1]
    both = cotangents_ref.shape[0]
    down = ADAPTER_SCALE * dot_first(tokens_ref[:, all_rows:], inputs_ref[...])
    cotangents = cotangents_ref[...]
    if wide - own_width > both:
        empty = jnp.zeros((wide - own_width - both, cotangents.shape[1]), jnp.bfloat16)
        cotangents = jnp.concatenate([cotangents, empty], axis=0)
    up = lax.dot_general(
        tokens_ref[:, :all_rows],
        cotangents,
        (((0,), (1,)), ((), ())),
        preferred_element_type=jnp.float32,
    )
    lane_kind = lax.broadcasted_iota(jnp.int32, up.shape, 1) // (both // 2)
    up = jnp.where(lane_kind == kind_of_row(up.shape, own_rank), ADAPTER_SCALE * up, 0.0)
    down = down.astype(jnp.bfloat16)
    up = up.astype(jnp.bfloat16)
    for group in range(groups):
        rows = slice(group * own_rows, (group + 1) * own_rows)
        out_ref[group, :, :own_width] = down[rows]
        out_ref[group, :, own_width:] = up[rows]


def update_factors(
    parts_ref,
    down_ref,
    down_first_ref,
    down_second_ref,
    up_ref,
    up_first_ref,
    up_second_ref,
    fresh_down_ref,
    fresh_down_first_ref,
    fresh_down_second_ref,
    fresh_up_ref,
    fresh_up_first_ref,
    fresh_up_second_ref,
    out_ref,
):
    groups = out_ref.shape[0]
    own_rank, own_width = down_ref.shape[1:]
    gradient = jnp.sum(parts_ref[...].astype(jnp.float32), axis=0)
    down = optimizer_update(
        stack_kinds(down_ref),
        gradient[:, :own_width],
        stack_kinds(down_first_ref),
        stack_kinds(down_second_ref),
    )
    up = optimizer_update(
        up_ref[...], gradient[:, own_width:], up_first_ref[...], up_second_ref[...]
    )
    for ref, values in zip(
        (fresh_down_ref, fresh_down_first_ref, fresh_down_second_ref), down
    ):
        for kind in range(2):
            ref[kind] = values[kind * own_rank : (kind + 1) * own_rank]
    for ref, values in zip((fresh_up_ref, fresh_up_first_ref, fresh_up_second_ref), up):
        ref[...] = values
    block = jnp.concatenate([down[0], up[0]], axis=1).astype(jnp.bfloat16)
    for group in range(groups):
        out_ref[group] = block


def send_rank_space(factors_ref, inputs_ref, out_ref, own_lines):
    ranks, height, _ = out_ref.shape
    own_columns = height - 2 * own_lines
    own_width = inputs_ref.shape[1]
    values = dot_last(inputs_ref[...], factors_ref[:, :own_width])
    high = values.astype(jnp.bfloat16).astype(jnp.float32)
    low = values - high
    up = factors_ref[:, own_width:].astype(jnp.float32).T
    up = (up[:own_columns] + up[own_columns : 2 * own_columns]).astype(jnp.bfloat16)
    for rank in range(ranks):
        rows = slice(rank * own_lines, (rank + 1) * own_lines)
        both = jnp.concatenate([high[rows], low[rows]], axis=0)
        out_ref[rank, : 2 * own_lines] = both.astype(jnp.bfloat16)
        out_ref[rank, 2 * own_lines :] = up


def cached_attention(lengths_ref, query_ref, key_ref, value_ref, peak_ref, total_ref, sum_ref):
    row_count, heads, slots, size = key_ref.shape
    lines = query_ref.shape[1]
    steps = 4
    line = lax.broadcasted_iota(jnp.int32, (lines, slots), 0) // steps % row_count
    slot = lax.broadcasted_iota(jnp.int32, (lines, slots), 1)
    valid = [(line == row) & (slot < lengths_ref[row]) for row in range(row_count)]
    for head in range(heads):
        query = query_ref[head]
        scores = jnp.full((lines, slots), MASKED, jnp.float32)
        for row in range(row_count):
            found = dot_last(query, key_ref[row, head]) * (1.0 / math.sqrt(size))
            scores = jnp.where(valid[row], found, scores)
        peak = jnp.max(scores, axis=1, keepdims=True)
        weights = jnp.exp(scores - peak)
        result = jnp.zeros((lines, size), jnp.float32)
        for row in range(row_count):
            own = jnp.where(valid[row], weights, 0.0).astype(jnp.bfloat16)
            result += jnp.dot(own, value_ref[row, head], preferred_element_type=jnp.float32)
        peak_ref[head] = peak
        total_ref[head] = jnp.sum(weights, axis=1, keepdims=True)
        sum_ref[head] = result


def finish(
    last_ref,
    frozen_ref,
    cosine_ref,
    sine_ref,
    query_ref,
    peak_ref,
    total_ref,
    sum_ref,
    attended_ref,
    keys_ref,
    values_ref,
    own_rank,
):
    row_count, steps, _ = keys_ref.shape
    heads, lines, size = query_ref.shape
    own_lines = row_count * steps
    ranks, _, all_rows = last_ref.shape
    parts = jnp.sum(last_ref[:, : 2 * own_lines, :].astype(jnp.float32), axis=0)
    rank_space = parts[:own_lines] + parts[own_lines:]
    full_up = last_ref[:, 2 * own_lines :, :].reshape(-1, all_rows)
    columns = full_up.shape[0]
    adapter_row = lax.broadcasted_iota(jnp.int32, (own_lines, all_rows), 1)
    raw = []
    for kind in range(2):
        own = jnp.where(adapter_row // own_rank % 2 == kind, rank_space, 0.0)
        high = own.astype(jnp.bfloat16).astype(jnp.float32)
        both = jnp.concatenate([high, own - high], axis=0).astype(jnp.bfloat16)
        both = dot_last(both, full_up)
        raw.append(
            frozen_ref[:, kind * columns : (kind + 1) * columns]
            + ADAPTER_SCALE * (both[:own_lines] + both[own_lines:])
        )
    for row in range(row_count):
        values_ref[row] = raw[1][row * steps : (row + 1) * steps]

    line = lax.broadcasted_iota(jnp.int32, (lines, 2 * own_lines), 0)
    entry = lax.broadcasted_iota(jnp.int32, (lines, 2 * own_lines), 1)
    valid = (line // steps % row_count == entry // steps) & (entry % steps <= line % steps)
    for head in range(heads):
        lanes = slice(head * size, (head + 1) * size)
        vector = raw[0][:, lanes]
        turned = pltpu.roll(vector, size // 2, 1)
        rotated = vector * cosine_ref[...] + turned * sine_ref[...]
        for row in range(row_count):
            keys_ref[row, :, lanes] = rotated[row * steps : (row + 1) * steps]
        fresh_keys = jnp.concatenate([rotated, rotated], axis=0).astype(jnp.bfloat16)
        fresh_values = jnp.concatenate([raw[1][:, lanes]] * 2, axis=0).astype(jnp.bfloat16)
        scores = dot_last(query_ref[head], fresh_keys) * (1.0 / math.sqrt(size))
        scores = jnp.where(valid, scores, MASKED)
        peak = jnp.maximum(peak_ref[head], jnp.max(scores, axis=1, keepdims=True))
        scale = jnp.exp(peak_ref[head] - peak)
        weights = jnp.where(valid, jnp.exp(scores - peak), 0.0)
        total = total_ref[head] * scale + jnp.sum(weights, axis=1, keepdims=True)
        result = sum_ref[head] * scale + jnp.dot(
            weights.astype(jnp.bfloat16), fresh_values, preferred_element_type=jnp.float32
        )
        result = result * (1.0 / total)
        group = lines // own_lines
        for query_head in range(group):
            at = (head * group + query_head) * size
            for row in range(row_count):
                start = query_head * own_lines + row * steps
                attended_ref[row, :, at : at + size] = result[start : start + steps]


def body(
    groups,
    ranks,
    trainer_token_inputs,
    weighted_output_cotangents,
    adapter_down_master,
    adapter_up_master,
    down_first_moment,
    down_second_moment,
    up_first_moment,
    up_second_moment,
    frozen_weights,
    decode_step_inputs,
    queries,
    rotated_key_cache,
    stored_value_cache,
    lengths,
):
    row_count, steps_count, query_width = queries.shape
    head_groups, cache_slots, head_size = rotated_key_cache.shape[1:]
    kinds, own_rank, own_width = adapter_down_master.shape
    own_columns, tokens = weighted_output_cotangents.shape[1:]
    columns = own_columns * ranks
    own_rows = kinds * own_rank
    all_rows = own_rows * groups
    own_lines = row_count * steps_count
    wide = own_width + -(-kinds * own_columns // 128) * 128

    def by_rank(values):
        return values.transpose(0, 2, 1)

    def placed(values):
        rest = wide - own_width - own_columns
        return jnp.concatenate(
            [
                jnp.pad(by_rank(values)[kind], ((0, 0), (at, rest - at)))
                for kind, at in ((0, 0), (1, own_columns))
            ]
        )

    def brought_back(values):
        blocks = [
            values[kind * own_rank : (kind + 1) * own_rank, at : at + own_columns]
            for kind, at in ((0, 0), (1, own_columns))
        ]
        return by_rank(jnp.stack(blocks))

    def call(kernel, outs, *operands):
        flops = 4 * max(operand.size for operand in operands)
        return pl.pallas_call(
            kernel,
            out_shape=outs,
            in_specs=[pl.BlockSpec(memory_space=pltpu.VMEM)] * len(operands),
            compiler_params=pltpu.CompilerParams(vmem_limit_bytes=KERNEL_BYTES),
            cost_estimate=pl.CostEstimate(
                flops=flops, bytes_accessed=flops, transcendentals=0
            ),
        )(*operands)

    def out(shape, kind=jnp.bfloat16):
        return jax.ShapeDtypeStruct(shape, kind)

    flat_inputs = decode_step_inputs.reshape(-1, own_width)

    sent = out((groups, own_rows, wide))
    masters = call(send_masters, sent, adapter_down_master, by_rank(adapter_up_master))
    later_inputs = after(flat_inputs, masters)
    frozen_part = jnp.concatenate(
        [product("rd,dc->rc", later_inputs, frozen_weights[kind]) for kind in range(kinds)], axis=1
    ).reshape(ranks, own_lines, kinds * columns)
    bits = ranks.bit_length() - 1
    frozen_part = frozen_part.reshape((2,) * bits + (own_lines, kinds * columns))
    factors = exchange(masters, "grp").reshape(all_rows, wide)

    frozen_part = half_sum(frozen_part, "tp", ranks, bits - 1, 0, earlier_sum=factors)
    frozen_part = half_sum(frozen_part, "tp", ranks, 1, bits - 2)

    lines = query_width // (head_groups * head_size) * own_lines
    query_lines = (
        after(queries, factors).reshape(row_count, steps_count, head_groups, -1, head_size)
        .transpose(2, 3, 0, 1, 4)
        .reshape(head_groups, lines, head_size)
    )
    column = jax.ShapeDtypeStruct((head_groups, lines, 1), jnp.float32)
    peak, total, cached = pl.pallas_call(
        cached_attention,
        out_shape=(
            column,
            column,
            jax.ShapeDtypeStruct((head_groups, lines, head_size), jnp.float32),
        ),
        in_specs=[pl.BlockSpec(memory_space=pltpu.SMEM)]
        + [pl.BlockSpec(memory_space=pltpu.VMEM)] * 3,
        compiler_params=pltpu.CompilerParams(vmem_limit_bytes=KERNEL_BYTES),
        cost_estimate=pl.CostEstimate(
            flops=8 * lines * cache_slots * head_size * head_groups,
            bytes_accessed=4 * row_count * head_groups * cache_slots * head_size,
            transcendentals=lines * cache_slots * head_groups,
        ),
    )(lengths, query_lines, rotated_key_cache, stored_value_cache)

    cotangents = weighted_output_cotangents.reshape(-1, tokens)
    shares = call(
        project_tokens, out((tokens, 2 * all_rows)), factors, trainer_token_inputs, cotangents
    ).reshape(ranks, -1, 2 * all_rows)
    sums = call(sum_tokens, out(shares.shape), exchange(shares, "tp"))
    sums, peak, total, cached = lax.optimization_barrier((sums, peak, total, cached))
    token_sums = exchange(sums, "tp").reshape(tokens, 2 * all_rows)

    gradients = call(
        functools.partial(send_gradients, own_rank=own_rank),
        sent,
        token_sums,
        trainer_token_inputs,
        cotangents,
    )
    frozen_part = half_sum(frozen_part, "tp", ranks, 0, bits - 1, earlier_send=gradients)
    own = out(adapter_down_master.shape, jnp.float32)
    small = out((own_rows, wide - own_width), jnp.float32)
    *fresh, fresh_factors = call(
        update_factors,
        (own, own, own, small, small, small, sent),
        exchange(gradients, "grp"),
        adapter_down_master,
        down_first_moment,
        down_second_moment,
        placed(adapter_up_master),
        placed(up_first_moment),
        placed(up_second_moment),
    )
    frozen_sum = half_sum(frozen_part, "tp", ranks, 0, 1, earlier_send=fresh_factors)
    factors = exchange(fresh_factors, "grp").reshape(all_rows, wide)

    rank_space = call(
        functools.partial(send_rank_space, own_lines=own_lines),
        out((ranks, 2 * own_lines + own_columns, all_rows)),
        factors,
        flat_inputs,
    )

    positions = lengths[:, None] + jnp.arange(steps_count, dtype=jnp.int32)[None, :]
    angles = positions.astype(jnp.float32).reshape(-1, 1) * rope_frequencies(head_size)
    cosine, sine = jnp.cos(angles), jnp.sin(angles)
    cosine = jnp.concatenate([cosine, cosine], axis=1)
    sine = jnp.concatenate([-sine, sine], axis=1)

    rank_space, frozen_sum = lax.optimization_barrier((rank_space, frozen_sum))
    last = exchange(rank_space, "tp")
    entries = jax.ShapeDtypeStruct((row_count, steps_count, columns), jnp.float32)
    attended, new_keys, new_values = pl.pallas_call(
        functools.partial(finish, own_rank=own_rank),
        out_shape=(jax.ShapeDtypeStruct(queries.shape, jnp.float32), entries, entries),
        in_specs=[pl.BlockSpec(memory_space=pltpu.VMEM)] * 8,
        compiler_params=pltpu.CompilerParams(vmem_limit_bytes=KERNEL_BYTES),
        cost_estimate=pl.CostEstimate(
            flops=4 * lines * own_lines * head_size * head_groups,
            bytes_accessed=4 * queries.size,
            transcendentals=lines * own_lines * head_groups,
        ),
    )(last, frozen_sum, cosine, sine, query_lines, peak, total, cached)

    return (
        attended,
        new_keys,
        new_values,
        fresh[0],
        brought_back(fresh[3]),
        fresh[1],
        fresh[2],
        brought_back(fresh[4]),
        brought_back(fresh[5]),
    )


def solution(mesh):
    in_specs = (
        P("grp", "tp"),
        P(None, "tp", "grp"),
        P(None, "grp", "tp"),
        P(None, "tp", "grp"),
        P(None, "grp", "tp"),
        P(None, "grp", "tp"),
        P(None, "tp", "grp"),
        P(None, "tp", "grp"),
        P(None, "tp", None),
        P("grp", None, "tp"),
        P(("grp", "tp"), None, None),
        P(("grp", "tp"), None, None, None),
        P(("grp", "tp"), None, None, None),
        P(("grp", "tp")),
    )
    out_specs = (
        P(("grp", "tp"), None, None),
        P(("grp", "tp"), None, None),
        P(("grp", "tp"), None, None),
        P(None, "grp", "tp"),
        P(None, "tp", "grp"),
        P(None, "grp", "tp"),
        P(None, "grp", "tp"),
        P(None, "tp", "grp"),
        P(None, "tp", "grp"),
    )
    placed = functools.partial(body, mesh.shape["grp"], mesh.shape["tp"])
    return jax.shard_map(placed, mesh=mesh, in_specs=in_specs, out_specs=out_specs, check_vma=False)
```

```python
import functools
import math

import jax
import jax.numpy as jnp
from jax import lax
from jax.experimental import pallas as pl
from jax.experimental.pallas import tpu as pltpu
from jax.sharding import PartitionSpec as P

OPT_STEP = 20


ADAPTER_SCALE = 2.0
LEARN_RATE = 0.001
WEIGHT_DECAY = 0.01
BETA_FIRST = 0.9
BETA_SECOND = 0.95
EPSILON = 1e-08
THETA = 500000.0
ROPE_FACTOR = 8.0
LOW_FACTOR = 1.0
HIGH_FACTOR = 4.0
INITIAL_CONTEXT = 8192.0
MASKED = -1e30
KERNEL_BYTES = 8 * 1024 * 1024


def rope_frequencies(head_size):
    half_head = head_size // 2
    exponent = jnp.arange(half_head, dtype=jnp.float32) * (2.0 / head_size)
    base_frequency = jnp.power(jnp.float32(THETA), -exponent)
    wavelength = 2.0 * math.pi / base_frequency
    smooth = (INITIAL_CONTEXT / wavelength - LOW_FACTOR) / (HIGH_FACTOR - LOW_FACTOR)
    blended = (1.0 - smooth) * base_frequency / ROPE_FACTOR + smooth * base_frequency
    scaled = jnp.where(
        wavelength > INITIAL_CONTEXT / LOW_FACTOR, base_frequency / ROPE_FACTOR, blended
    )
    return jnp.where(wavelength < INITIAL_CONTEXT / HIGH_FACTOR, base_frequency, scaled)


def optimizer_update(current, gradient, moment_mean, moment_square):
    mean_next = BETA_FIRST * moment_mean + (1.0 - BETA_FIRST) * gradient
    square_next = BETA_SECOND * moment_square + (1.0 - BETA_SECOND) * gradient * gradient
    bias_first = 1.0 - BETA_FIRST**OPT_STEP
    bias_second = 1.0 - BETA_SECOND**OPT_STEP
    update = mean_next / bias_first / (jnp.sqrt(square_next / bias_second) + EPSILON)
    return (current - LEARN_RATE * (update + WEIGHT_DECAY * current), mean_next, square_next)


def exchange(pieces, axis):
    return lax.all_to_all(pieces, axis, 0, 0, tiled=True)


def product(spec, left, right):
    return jnp.einsum(spec, left, right, preferred_element_type=jnp.float32)


def after(values, earlier):
    return lax.optimization_barrier((values, earlier))[0]


def half_sum(values, axis, count, at, bit, earlier_sum=None, earlier_send=None, kind=jnp.float32):
    if earlier_send is not None:
        values = after(values, earlier_send)
    low = lax.index_in_dim(values, 0, at, keepdims=False)
    high = lax.index_in_dim(values, 1, at, keepdims=False)
    upper = (lax.axis_index(axis) >> bit) & 1 == 1
    pairs = [(place, place ^ (1 << bit)) for place in range(count)]
    arrived = lax.ppermute(jnp.where(upper, low, high).astype(kind), axis, pairs)
    kept = jnp.where(upper, high, low)
    if earlier_sum is not None:
        kept = after(kept, earlier_sum)
    return kept + arrived.astype(jnp.float32)


def dot_last(left, right):
    return lax.dot_general(
        left, right, (((1,), (1,)), ((), ())), preferred_element_type=jnp.float32
    )


def dot_first(left, right):
    return lax.dot_general(
        left, right, (((0,), (0,)), ((), ())), preferred_element_type=jnp.float32
    )


def kind_of_row(shape, own_rank):
    return lax.broadcasted_iota(jnp.int32, shape, 0) // own_rank % 2


def stack_kinds(ref):
    return jnp.concatenate([ref[0], ref[1]], axis=0)


def send_masters(down_ref, up_ref, out_ref):
    groups, _, wide = out_ref.shape
    own_rank, own_width = down_ref.shape[1:]
    own_columns = up_ref.shape[2]
    rest = wide - own_width
    rows = []
    for kind in range(2):
        line = up_ref[kind]
        before = jnp.zeros((own_rank, kind * own_columns), jnp.float32)
        after = jnp.zeros((own_rank, rest - (kind + 1) * own_columns), jnp.float32)
        parts = [part for part in (before, line, after) if part.shape[1]]
        rows.append(jnp.concatenate(parts, axis=1))
    block = jnp.concatenate([stack_kinds(down_ref), jnp.concatenate(rows, axis=0)], axis=1)
    block = block.astype(jnp.bfloat16)
    for group in range(groups):
        out_ref[group] = block


def project_tokens(factors_ref, inputs_ref, cotangents_ref, out_ref):
    all_rows = factors_ref.shape[0]
    own_width = inputs_ref.shape[1]
    both = cotangents_ref.shape[0]
    projected = dot_last(inputs_ref[...], factors_ref[:, :own_width])
    pulled = lax.dot_general(
        cotangents_ref[...],
        factors_ref[:, own_width : own_width + both],
        (((0,), (1,)), ((), ())),
        preferred_element_type=jnp.float32,
    )
    out_ref[:, :all_rows] = projected.astype(jnp.bfloat16)
    out_ref[:, all_rows:] = pulled.astype(jnp.bfloat16)


def sum_tokens(parts_ref, out_ref):
    total = jnp.sum(parts_ref[...].astype(jnp.float32), axis=0).astype(jnp.bfloat16)
    for rank in range(out_ref.shape[0]):
        out_ref[rank] = total


def send_gradients(tokens_ref, inputs_ref, cotangents_ref, out_ref, own_rank):
    groups, own_rows, wide = out_ref.shape
    all_rows = groups * own_rows
    own_width = inputs_ref.shape[1]
    both = cotangents_ref.shape[0]
    down = ADAPTER_SCALE * dot_first(tokens_ref[:, all_rows:], inputs_ref[...])
    cotangents = cotangents_ref[...]
    if wide - own_width > both:
        empty = jnp.zeros((wide - own_width - both, cotangents.shape[1]), jnp.bfloat16)
        cotangents = jnp.concatenate([cotangents, empty], axis=0)
    up = lax.dot_general(
        tokens_ref[:, :all_rows],
        cotangents,
        (((0,), (1,)), ((), ())),
        preferred_element_type=jnp.float32,
    )
    lane_kind = lax.broadcasted_iota(jnp.int32, up.shape, 1) // (both // 2)
    up = jnp.where(lane_kind == kind_of_row(up.shape, own_rank), ADAPTER_SCALE * up, 0.0)
    down = down.astype(jnp.bfloat16)
    up = up.astype(jnp.bfloat16)
    for group in range(groups):
        rows = slice(group * own_rows, (group + 1) * own_rows)
        out_ref[group, :, :own_width] = down[rows]
        out_ref[group, :, own_width:] = up[rows]


def update_factors(
    parts_ref,
    down_ref,
    down_first_ref,
    down_second_ref,
    up_ref,
    up_first_ref,
    up_second_ref,
    fresh_down_ref,
    fresh_down_first_ref,
    fresh_down_second_ref,
    fresh_up_ref,
    fresh_up_first_ref,
    fresh_up_second_ref,
    out_ref,
):
    groups = out_ref.shape[0]
    own_rank, own_width = down_ref.shape[1:]
    gradient = jnp.sum(parts_ref[...].astype(jnp.float32), axis=0)
    down = optimizer_update(
        stack_kinds(down_ref),
        gradient[:, :own_width],
        stack_kinds(down_first_ref),
        stack_kinds(down_second_ref),
    )
    up = optimizer_update(
        up_ref[...], gradient[:, own_width:], up_first_ref[...], up_second_ref[...]
    )
    for ref, values in zip(
        (fresh_down_ref, fresh_down_first_ref, fresh_down_second_ref), down
    ):
        for kind in range(2):
            ref[kind] = values[kind * own_rank : (kind + 1) * own_rank]
    for ref, values in zip((fresh_up_ref, fresh_up_first_ref, fresh_up_second_ref), up):
        ref[...] = values
    block = jnp.concatenate([down[0], up[0]], axis=1).astype(jnp.bfloat16)
    for group in range(groups):
        out_ref[group] = block


def send_rank_space(factors_ref, inputs_ref, out_ref, own_lines):
    ranks, height, _ = out_ref.shape
    own_columns = height - 2 * own_lines
    own_width = inputs_ref.shape[1]
    values = dot_last(inputs_ref[...], factors_ref[:, :own_width])
    high = values.astype(jnp.bfloat16).astype(jnp.float32)
    low = values - high
    up = factors_ref[:, own_width:].astype(jnp.float32).T
    up = (up[:own_columns] + up[own_columns : 2 * own_columns]).astype(jnp.bfloat16)
    for rank in range(ranks):
        rows = slice(rank * own_lines, (rank + 1) * own_lines)
        both = jnp.concatenate([high[rows], low[rows]], axis=0)
        out_ref[rank, : 2 * own_lines] = both.astype(jnp.bfloat16)
        out_ref[rank, 2 * own_lines :] = up


def cached_attention(lengths_ref, query_ref, key_ref, value_ref, peak_ref, total_ref, sum_ref):
    row_count, heads, slots, size = key_ref.shape
    lines = query_ref.shape[1]
    steps = 4
    line = lax.broadcasted_iota(jnp.int32, (lines, slots), 0) // steps % row_count
    slot = lax.broadcasted_iota(jnp.int32, (lines, slots), 1)
    valid = [(line == row) & (slot < lengths_ref[row]) for row in range(row_count)]
    for head in range(heads):
        query = query_ref[head]
        scores = jnp.full((lines, slots), MASKED, jnp.float32)
        for row in range(row_count):
            found = dot_last(query, key_ref[row, head]) * (1.0 / math.sqrt(size))
            scores = jnp.where(valid[row], found, scores)
        peak = jnp.max(scores, axis=1, keepdims=True)
        weights = jnp.exp(scores - peak)
        result = jnp.zeros((lines, size), jnp.float32)
        for row in range(row_count):
            own = jnp.where(valid[row], weights, 0.0).astype(jnp.bfloat16)
            result += jnp.dot(own, value_ref[row, head], preferred_element_type=jnp.float32)
        peak_ref[head] = peak
        total_ref[head] = jnp.sum(weights, axis=1, keepdims=True)
        sum_ref[head] = result


def finish(
    last_ref,
    frozen_ref,
    cosine_ref,
    sine_ref,
    query_ref,
    peak_ref,
    total_ref,
    sum_ref,
    attended_ref,
    keys_ref,
    values_ref,
    own_rank,
):
    row_count, steps, _ = keys_ref.shape
    heads, lines, size = query_ref.shape
    own_lines = row_count * steps
    ranks, _, all_rows = last_ref.shape
    parts = jnp.sum(last_ref[:, : 2 * own_lines, :].astype(jnp.float32), axis=0)
    rank_space = parts[:own_lines] + parts[own_lines:]
    full_up = last_ref[:, 2 * own_lines :, :].reshape(-1, all_rows)
    columns = full_up.shape[0]
    adapter_row = lax.broadcasted_iota(jnp.int32, (own_lines, all_rows), 1)
    raw = []
    for kind in range(2):
        own = jnp.where(adapter_row // own_rank % 2 == kind, rank_space, 0.0)
        high = own.astype(jnp.bfloat16).astype(jnp.float32)
        both = jnp.concatenate([high, own - high], axis=0).astype(jnp.bfloat16)
        both = dot_last(both, full_up)
        raw.append(
            frozen_ref[:, kind * columns : (kind + 1) * columns]
            + ADAPTER_SCALE * (both[:own_lines] + both[own_lines:])
        )
    for row in range(row_count):
        values_ref[row] = raw[1][row * steps : (row + 1) * steps]

    line = lax.broadcasted_iota(jnp.int32, (lines, 2 * own_lines), 0)
    entry = lax.broadcasted_iota(jnp.int32, (lines, 2 * own_lines), 1)
    valid = (line // steps % row_count == entry // steps) & (entry % steps <= line % steps)
    for head in range(heads):
        lanes = slice(head * size, (head + 1) * size)
        vector = raw[0][:, lanes]
        turned = pltpu.roll(vector, size // 2, 1)
        rotated = vector * cosine_ref[...] + turned * sine_ref[...]
        for row in range(row_count):
            keys_ref[row, :, lanes] = rotated[row * steps : (row + 1) * steps]
        fresh_keys = jnp.concatenate([rotated, rotated], axis=0).astype(jnp.bfloat16)
        fresh_values = jnp.concatenate([raw[1][:, lanes]] * 2, axis=0).astype(jnp.bfloat16)
        scores = dot_last(query_ref[head], fresh_keys) * (1.0 / math.sqrt(size))
        scores = jnp.where(valid, scores, MASKED)
        peak = jnp.maximum(peak_ref[head], jnp.max(scores, axis=1, keepdims=True))
        scale = jnp.exp(peak_ref[head] - peak)
        weights = jnp.where(valid, jnp.exp(scores - peak), 0.0)
        total = total_ref[head] * scale + jnp.sum(weights, axis=1, keepdims=True)
        result = sum_ref[head] * scale + jnp.dot(
            weights.astype(jnp.bfloat16), fresh_values, preferred_element_type=jnp.float32
        )
        result = result * (1.0 / total)
        group = lines // own_lines
        for query_head in range(group):
            at = (head * group + query_head) * size
            for row in range(row_count):
                start = query_head * own_lines + row * steps
                attended_ref[row, :, at : at + size] = result[start : start + steps]


def body(
    groups,
    ranks,
    trainer_token_inputs,
    weighted_output_cotangents,
    adapter_down_master,
    adapter_up_master,
    down_first_moment,
    down_second_moment,
    up_first_moment,
    up_second_moment,
    frozen_weights,
    decode_step_inputs,
    queries,
    rotated_key_cache,
    stored_value_cache,
    lengths,
):
    row_count, steps_count, query_width = queries.shape
    head_groups, cache_slots, head_size = rotated_key_cache.shape[1:]
    kinds, own_rank, own_width = adapter_down_master.shape
    own_columns, tokens = weighted_output_cotangents.shape[1:]
    columns = own_columns * ranks
    own_rows = kinds * own_rank
    all_rows = own_rows * groups
    own_lines = row_count * steps_count
    wide = own_width + -(-kinds * own_columns // 128) * 128

    def by_rank(values):
        return values.transpose(0, 2, 1)

    def placed(values):
        rest = wide - own_width - own_columns
        return jnp.concatenate(
            [
                jnp.pad(by_rank(values)[kind], ((0, 0), (at, rest - at)))
                for kind, at in ((0, 0), (1, own_columns))
            ]
        )

    def brought_back(values):
        blocks = [
            values[kind * own_rank : (kind + 1) * own_rank, at : at + own_columns]
            for kind, at in ((0, 0), (1, own_columns))
        ]
        return by_rank(jnp.stack(blocks))

    def call(kernel, outs, *operands, limit=KERNEL_BYTES):
        flops = 4 * max(operand.size for operand in operands)
        return pl.pallas_call(
            kernel,
            out_shape=outs,
            in_specs=[pl.BlockSpec(memory_space=pltpu.VMEM)] * len(operands),
            compiler_params=pltpu.CompilerParams(vmem_limit_bytes=limit),
            cost_estimate=pl.CostEstimate(
                flops=flops, bytes_accessed=flops, transcendentals=0
            ),
        )(*operands)

    def out(shape, kind=jnp.bfloat16):
        return jax.ShapeDtypeStruct(shape, kind)

    flat_inputs = decode_step_inputs.reshape(-1, own_width)

    sent = out((groups, own_rows, wide))
    masters = call(
        send_masters, sent, adapter_down_master, by_rank(adapter_up_master), limit=None
    )
    later_inputs = after(flat_inputs, masters)
    frozen_part = jnp.concatenate(
        [product("rd,dc->rc", later_inputs, frozen_weights[kind]) for kind in range(kinds)], axis=1
    ).reshape(ranks, own_lines, kinds * columns)
    bits = ranks.bit_length() - 1
    frozen_part = frozen_part.reshape((2,) * bits + (own_lines, kinds * columns))
    factors = exchange(masters, "grp").reshape(all_rows, wide)

    frozen_part = half_sum(frozen_part, "tp", ranks, bits - 1, 0, earlier_sum=factors)
    frozen_part = half_sum(frozen_part, "tp", ranks, 1, bits - 2)

    lines = query_width // (head_groups * head_size) * own_lines
    query_lines = (
        after(queries, factors).reshape(row_count, steps_count, head_groups, -1, head_size)
        .transpose(2, 3, 0, 1, 4)
        .reshape(head_groups, lines, head_size)
    )
    column = jax.ShapeDtypeStruct((head_groups, lines, 1), jnp.float32)
    peak, total, cached = pl.pallas_call(
        cached_attention,
        out_shape=(
            column,
            column,
            jax.ShapeDtypeStruct((head_groups, lines, head_size), jnp.float32),
        ),
        in_specs=[pl.BlockSpec(memory_space=pltpu.SMEM)]
        + [pl.BlockSpec(memory_space=pltpu.VMEM)] * 3,
        compiler_params=pltpu.CompilerParams(vmem_limit_bytes=KERNEL_BYTES),
        cost_estimate=pl.CostEstimate(
            flops=8 * lines * cache_slots * head_size * head_groups,
            bytes_accessed=4 * row_count * head_groups * cache_slots * head_size,
            transcendentals=lines * cache_slots * head_groups,
        ),
    )(lengths, query_lines, rotated_key_cache, stored_value_cache)

    cotangents = weighted_output_cotangents.reshape(-1, tokens)
    shares = call(
        project_tokens, out((tokens, 2 * all_rows)), factors, trainer_token_inputs, cotangents
    ).reshape(ranks, -1, 2 * all_rows)
    sums = call(sum_tokens, out(shares.shape), exchange(shares, "tp"))
    sums, peak, total, cached = lax.optimization_barrier((sums, peak, total, cached))
    token_sums = exchange(sums, "tp").reshape(tokens, 2 * all_rows)

    gradients = call(
        functools.partial(send_gradients, own_rank=own_rank),
        sent,
        token_sums,
        trainer_token_inputs,
        cotangents,
    )
    own = out(adapter_down_master.shape, jnp.float32)
    small = out((own_rows, wide - own_width), jnp.float32)
    *fresh, fresh_factors = call(
        update_factors,
        (own, own, own, small, small, small, sent),
        exchange(gradients, "grp"),
        adapter_down_master,
        down_first_moment,
        down_second_moment,
        placed(adapter_up_master),
        placed(up_first_moment),
        placed(up_second_moment),
    )
    frozen_part = half_sum(
        frozen_part,
        "tp",
        ranks,
        1,
        1,
        earlier_sum=fresh_factors,
        earlier_send=gradients,
        kind=jnp.bfloat16,
    )
    frozen_sum = half_sum(frozen_part, "tp", ranks, 0, bits - 1)
    factors = exchange(fresh_factors, "grp").reshape(all_rows, wide)

    rank_space = call(
        functools.partial(send_rank_space, own_lines=own_lines),
        out((ranks, 2 * own_lines + own_columns, all_rows)),
        factors,
        flat_inputs,
    )

    positions = lengths[:, None] + jnp.arange(steps_count, dtype=jnp.int32)[None, :]
    angles = positions.astype(jnp.float32).reshape(-1, 1) * rope_frequencies(head_size)
    cosine, sine = jnp.cos(angles), jnp.sin(angles)
    cosine = jnp.concatenate([cosine, cosine], axis=1)
    sine = jnp.concatenate([-sine, sine], axis=1)

    rank_space, frozen_sum = lax.optimization_barrier((rank_space, frozen_sum))
    last = exchange(rank_space, "tp")
    entries = jax.ShapeDtypeStruct((row_count, steps_count, columns), jnp.float32)
    attended, new_keys, new_values = pl.pallas_call(
        functools.partial(finish, own_rank=own_rank),
        out_shape=(jax.ShapeDtypeStruct(queries.shape, jnp.float32), entries, entries),
        in_specs=[pl.BlockSpec(memory_space=pltpu.VMEM)] * 8,
        compiler_params=pltpu.CompilerParams(vmem_limit_bytes=KERNEL_BYTES),
        cost_estimate=pl.CostEstimate(
            flops=4 * lines * own_lines * head_size * head_groups,
            bytes_accessed=4 * queries.size,
            transcendentals=lines * own_lines * head_groups,
        ),
    )(last, frozen_sum, cosine, sine, query_lines, peak, total, cached)

    return (
        attended,
        new_keys,
        new_values,
        fresh[0],
        brought_back(fresh[3]),
        fresh[1],
        fresh[2],
        brought_back(fresh[4]),
        brought_back(fresh[5]),
    )


def solution(mesh):
    in_specs = (
        P("grp", "tp"),
        P(None, "tp", "grp"),
        P(None, "grp", "tp"),
        P(None, "tp", "grp"),
        P(None, "grp", "tp"),
        P(None, "grp", "tp"),
        P(None, "tp", "grp"),
        P(None, "tp", "grp"),
        P(None, "tp", None),
        P("grp", None, "tp"),
        P(("grp", "tp"), None, None),
        P(("grp", "tp"), None, None, None),
        P(("grp", "tp"), None, None, None),
        P(("grp", "tp")),
    )
    out_specs = (
        P(("grp", "tp"), None, None),
        P(("grp", "tp"), None, None),
        P(("grp", "tp"), None, None),
        P(None, "grp", "tp"),
        P(None, "tp", "grp"),
        P(None, "grp", "tp"),
        P(None, "grp", "tp"),
        P(None, "tp", "grp"),
        P(None, "tp", "grp"),
    )
    placed = functools.partial(body, mesh.shape["grp"], mesh.shape["tp"])
    return jax.shard_map(placed, mesh=mesh, in_specs=in_specs, out_specs=out_specs, check_vma=False)
```

```python
import functools
import math

import jax
import jax.numpy as jnp
from jax import lax
from jax.experimental import pallas as pl
from jax.experimental.pallas import tpu as pltpu
from jax.sharding import PartitionSpec as P

OPT_STEP = 20


ADAPTER_SCALE = 2.0
LEARN_RATE = 0.001
WEIGHT_DECAY = 0.01
BETA_FIRST = 0.9
BETA_SECOND = 0.95
EPSILON = 1e-08
THETA = 500000.0
ROPE_FACTOR = 8.0
LOW_FACTOR = 1.0
HIGH_FACTOR = 4.0
INITIAL_CONTEXT = 8192.0
MASKED = -1e30
KERNEL_BYTES = 8 * 1024 * 1024


def rope_frequencies(head_size):
    half_head = head_size // 2
    exponent = jnp.arange(half_head, dtype=jnp.float32) * (2.0 / head_size)
    base_frequency = jnp.power(jnp.float32(THETA), -exponent)
    wavelength = 2.0 * math.pi / base_frequency
    smooth = (INITIAL_CONTEXT / wavelength - LOW_FACTOR) / (HIGH_FACTOR - LOW_FACTOR)
    blended = (1.0 - smooth) * base_frequency / ROPE_FACTOR + smooth * base_frequency
    scaled = jnp.where(
        wavelength > INITIAL_CONTEXT / LOW_FACTOR, base_frequency / ROPE_FACTOR, blended
    )
    return jnp.where(wavelength < INITIAL_CONTEXT / HIGH_FACTOR, base_frequency, scaled)


def optimizer_update(current, gradient, moment_mean, moment_square):
    mean_next = BETA_FIRST * moment_mean + (1.0 - BETA_FIRST) * gradient
    square_next = BETA_SECOND * moment_square + (1.0 - BETA_SECOND) * gradient * gradient
    bias_first = 1.0 - BETA_FIRST**OPT_STEP
    bias_second = 1.0 - BETA_SECOND**OPT_STEP
    update = mean_next / bias_first / (jnp.sqrt(square_next / bias_second) + EPSILON)
    return (current - LEARN_RATE * (update + WEIGHT_DECAY * current), mean_next, square_next)


def exchange(pieces, axis):
    return lax.all_to_all(pieces, axis, 0, 0, tiled=True)


def product(spec, left, right):
    return jnp.einsum(spec, left, right, preferred_element_type=jnp.float32)


def after(values, earlier):
    return lax.optimization_barrier((values, earlier))[0]


def half_sum(values, axis, count, at, bit, earlier_sum=None, earlier_send=None, kind=jnp.float32):
    if earlier_send is not None:
        values = after(values, earlier_send)
    low = lax.index_in_dim(values, 0, at, keepdims=False)
    high = lax.index_in_dim(values, 1, at, keepdims=False)
    upper = (lax.axis_index(axis) >> bit) & 1 == 1
    pairs = [(place, place ^ (1 << bit)) for place in range(count)]
    arrived = lax.ppermute(jnp.where(upper, low, high).astype(kind), axis, pairs)
    kept = jnp.where(upper, high, low)
    if earlier_sum is not None:
        kept = after(kept, earlier_sum)
    return kept + arrived.astype(jnp.float32)


def dot_last(left, right):
    return lax.dot_general(
        left, right, (((1,), (1,)), ((), ())), preferred_element_type=jnp.float32
    )


def dot_first(left, right):
    return lax.dot_general(
        left, right, (((0,), (0,)), ((), ())), preferred_element_type=jnp.float32
    )


def kind_of_row(shape, own_rank):
    return lax.broadcasted_iota(jnp.int32, shape, 0) // own_rank % 2


def stack_kinds(ref):
    return jnp.concatenate([ref[0], ref[1]], axis=0)


def send_masters(down_ref, up_ref, out_ref):
    groups, _, wide = out_ref.shape
    own_rank, own_width = down_ref.shape[1:]
    own_columns = up_ref.shape[2]
    rest = wide - own_width
    rows = []
    for kind in range(2):
        line = up_ref[kind]
        before = jnp.zeros((own_rank, kind * own_columns), jnp.float32)
        after = jnp.zeros((own_rank, rest - (kind + 1) * own_columns), jnp.float32)
        parts = [part for part in (before, line, after) if part.shape[1]]
        rows.append(jnp.concatenate(parts, axis=1))
    block = jnp.concatenate([stack_kinds(down_ref), jnp.concatenate(rows, axis=0)], axis=1)
    block = block.astype(jnp.bfloat16)
    for group in range(groups):
        out_ref[group] = block


def project_decode(inputs_ref, weights_ref, out_ref):
    columns = weights_ref.shape[2]
    for kind in range(weights_ref.shape[0]):
        out_ref[:, kind * columns : (kind + 1) * columns] = jnp.dot(
            inputs_ref[...], weights_ref[kind], preferred_element_type=jnp.float32
        )


def project_tokens(factors_ref, inputs_ref, cotangents_ref, out_ref):
    all_rows = factors_ref.shape[0]
    own_width = inputs_ref.shape[1]
    both = cotangents_ref.shape[0]
    projected = dot_last(inputs_ref[...], factors_ref[:, :own_width])
    pulled = lax.dot_general(
        cotangents_ref[...],
        factors_ref[:, own_width : own_width + both],
        (((0,), (1,)), ((), ())),
        preferred_element_type=jnp.float32,
    )
    out_ref[:, :all_rows] = projected.astype(jnp.bfloat16)
    out_ref[:, all_rows:] = pulled.astype(jnp.bfloat16)


def sum_tokens(parts_ref, out_ref):
    total = jnp.sum(parts_ref[...].astype(jnp.float32), axis=0).astype(jnp.bfloat16)
    for rank in range(out_ref.shape[0]):
        out_ref[rank] = total


def send_gradients(tokens_ref, inputs_ref, cotangents_ref, out_ref, own_rank):
    groups, own_rows, wide = out_ref.shape
    all_rows = groups * own_rows
    own_width = inputs_ref.shape[1]
    both = cotangents_ref.shape[0]
    down = ADAPTER_SCALE * dot_first(tokens_ref[:, all_rows:], inputs_ref[...])
    cotangents = cotangents_ref[...]
    if wide - own_width > both:
        empty = jnp.zeros((wide - own_width - both, cotangents.shape[1]), jnp.bfloat16)
        cotangents = jnp.concatenate([cotangents, empty], axis=0)
    up = lax.dot_general(
        tokens_ref[:, :all_rows],
        cotangents,
        (((0,), (1,)), ((), ())),
        preferred_element_type=jnp.float32,
    )
    lane_kind = lax.broadcasted_iota(jnp.int32, up.shape, 1) // (both // 2)
    up = jnp.where(lane_kind == kind_of_row(up.shape, own_rank), ADAPTER_SCALE * up, 0.0)
    for group in range(groups):
        rows = slice(group * own_rows, (group + 1) * own_rows)
        out_ref[group, :, :own_width] = down[rows].astype(jnp.bfloat16)
        out_ref[group, :, own_width:] = up[rows].astype(jnp.bfloat16)


def update_factors(
    parts_ref,
    down_ref,
    down_first_ref,
    down_second_ref,
    up_ref,
    up_first_ref,
    up_second_ref,
    fresh_down_ref,
    fresh_down_first_ref,
    fresh_down_second_ref,
    fresh_up_ref,
    fresh_up_first_ref,
    fresh_up_second_ref,
    out_ref,
):
    groups = out_ref.shape[0]
    own_rank, own_width = down_ref.shape[1:]
    gradient = jnp.sum(parts_ref[...].astype(jnp.float32), axis=0)
    down = optimizer_update(
        stack_kinds(down_ref),
        gradient[:, :own_width],
        stack_kinds(down_first_ref),
        stack_kinds(down_second_ref),
    )
    up = optimizer_update(
        up_ref[...], gradient[:, own_width:], up_first_ref[...], up_second_ref[...]
    )
    for ref, values in zip(
        (fresh_down_ref, fresh_down_first_ref, fresh_down_second_ref), down
    ):
        for kind in range(2):
            ref[kind] = values[kind * own_rank : (kind + 1) * own_rank]
    for ref, values in zip((fresh_up_ref, fresh_up_first_ref, fresh_up_second_ref), up):
        ref[...] = values
    block = jnp.concatenate([down[0], up[0]], axis=1).astype(jnp.bfloat16)
    for group in range(groups):
        out_ref[group] = block


def send_rank_space(factors_ref, inputs_ref, out_ref, own_lines):
    ranks, height, _ = out_ref.shape
    own_columns = height - 2 * own_lines
    own_width = inputs_ref.shape[1]
    values = dot_last(inputs_ref[...], factors_ref[:, :own_width])
    high = values.astype(jnp.bfloat16).astype(jnp.float32)
    low = values - high
    up = factors_ref[:, own_width:].astype(jnp.float32).T
    up = (up[:own_columns] + up[own_columns : 2 * own_columns]).astype(jnp.bfloat16)
    for rank in range(ranks):
        rows = slice(rank * own_lines, (rank + 1) * own_lines)
        both = jnp.concatenate([high[rows], low[rows]], axis=0)
        out_ref[rank, : 2 * own_lines] = both.astype(jnp.bfloat16)
        out_ref[rank, 2 * own_lines :] = up


def cached_attention(lengths_ref, query_ref, key_ref, value_ref, peak_ref, total_ref, sum_ref):
    row_count, heads, slots, size = key_ref.shape
    lines = query_ref.shape[1]
    steps = 4
    line = lax.broadcasted_iota(jnp.int32, (lines, slots), 0) // steps % row_count
    slot = lax.broadcasted_iota(jnp.int32, (lines, slots), 1)
    valid = [(line == row) & (slot < lengths_ref[row]) for row in range(row_count)]
    for head in range(heads):
        query = query_ref[head]
        scores = jnp.full((lines, slots), MASKED, jnp.float32)
        for row in range(row_count):
            found = dot_last(query, key_ref[row, head]) * (1.0 / math.sqrt(size))
            scores = jnp.where(valid[row], found, scores)
        peak = jnp.max(scores, axis=1, keepdims=True)
        weights = jnp.exp(scores - peak)
        result = jnp.zeros((lines, size), jnp.float32)
        for row in range(row_count):
            own = jnp.where(valid[row], weights, 0.0).astype(jnp.bfloat16)
            result += jnp.dot(own, value_ref[row, head], preferred_element_type=jnp.float32)
        peak_ref[head] = peak
        total_ref[head] = jnp.sum(weights, axis=1, keepdims=True)
        sum_ref[head] = result


def finish(
    last_ref,
    frozen_ref,
    cosine_ref,
    sine_ref,
    query_ref,
    peak_ref,
    total_ref,
    sum_ref,
    attended_ref,
    keys_ref,
    values_ref,
    own_rank,
):
    row_count, steps, _ = keys_ref.shape
    heads, lines, size = query_ref.shape
    own_lines = row_count * steps
    ranks, _, all_rows = last_ref.shape
    parts = jnp.sum(last_ref[:, : 2 * own_lines, :].astype(jnp.float32), axis=0)
    rank_space = parts[:own_lines] + parts[own_lines:]
    full_up = last_ref[:, 2 * own_lines :, :].reshape(-1, all_rows)
    columns = full_up.shape[0]
    adapter_row = lax.broadcasted_iota(jnp.int32, (own_lines, all_rows), 1)
    raw = []
    for kind in range(2):
        own = jnp.where(adapter_row // own_rank % 2 == kind, rank_space, 0.0)
        high = own.astype(jnp.bfloat16).astype(jnp.float32)
        both = jnp.concatenate([high, own - high], axis=0).astype(jnp.bfloat16)
        both = dot_last(both, full_up)
        raw.append(
            frozen_ref[:, kind * columns : (kind + 1) * columns]
            + ADAPTER_SCALE * (both[:own_lines] + both[own_lines:])
        )
    for row in range(row_count):
        values_ref[row] = raw[1][row * steps : (row + 1) * steps]

    line = lax.broadcasted_iota(jnp.int32, (lines, 2 * own_lines), 0)
    entry = lax.broadcasted_iota(jnp.int32, (lines, 2 * own_lines), 1)
    valid = (line // steps % row_count == entry // steps) & (entry % steps <= line % steps)
    for head in range(heads):
        lanes = slice(head * size, (head + 1) * size)
        vector = raw[0][:, lanes]
        turned = pltpu.roll(vector, size // 2, 1)
        rotated = vector * cosine_ref[...] + turned * sine_ref[...]
        for row in range(row_count):
            keys_ref[row, :, lanes] = rotated[row * steps : (row + 1) * steps]
        fresh_keys = jnp.concatenate([rotated, rotated], axis=0).astype(jnp.bfloat16)
        fresh_values = jnp.concatenate([raw[1][:, lanes]] * 2, axis=0).astype(jnp.bfloat16)
        scores = dot_last(query_ref[head], fresh_keys) * (1.0 / math.sqrt(size))
        scores = jnp.where(valid, scores, MASKED)
        peak = jnp.maximum(peak_ref[head], jnp.max(scores, axis=1, keepdims=True))
        scale = jnp.exp(peak_ref[head] - peak)
        weights = jnp.where(valid, jnp.exp(scores - peak), 0.0)
        total = total_ref[head] * scale + jnp.sum(weights, axis=1, keepdims=True)
        result = sum_ref[head] * scale + jnp.dot(
            weights.astype(jnp.bfloat16), fresh_values, preferred_element_type=jnp.float32
        )
        result = result * (1.0 / total)
        group = lines // own_lines
        for query_head in range(group):
            at = (head * group + query_head) * size
            for row in range(row_count):
                start = query_head * own_lines + row * steps
                attended_ref[row, :, at : at + size] = result[start : start + steps]


def body(
    groups,
    ranks,
    trainer_token_inputs,
    weighted_output_cotangents,
    adapter_down_master,
    adapter_up_master,
    down_first_moment,
    down_second_moment,
    up_first_moment,
    up_second_moment,
    frozen_weights,
    decode_step_inputs,
    queries,
    rotated_key_cache,
    stored_value_cache,
    lengths,
):
    row_count, steps_count, query_width = queries.shape
    head_groups, cache_slots, head_size = rotated_key_cache.shape[1:]
    kinds, own_rank, own_width = adapter_down_master.shape
    own_columns, tokens = weighted_output_cotangents.shape[1:]
    columns = own_columns * ranks
    own_rows = kinds * own_rank
    all_rows = own_rows * groups
    own_lines = row_count * steps_count
    wide = own_width + -(-kinds * own_columns // 128) * 128

    def by_rank(values):
        return values.transpose(0, 2, 1)

    def placed(values):
        rest = wide - own_width - own_columns
        return jnp.concatenate(
            [
                jnp.pad(by_rank(values)[kind], ((0, 0), (at, rest - at)))
                for kind, at in ((0, 0), (1, own_columns))
            ]
        )

    def brought_back(values):
        blocks = [
            values[kind * own_rank : (kind + 1) * own_rank, at : at + own_columns]
            for kind, at in ((0, 0), (1, own_columns))
        ]
        return by_rank(jnp.stack(blocks))

    def call(kernel, outs, *operands, limit=KERNEL_BYTES):
        flops = 4 * max(operand.size for operand in operands)
        return pl.pallas_call(
            kernel,
            out_shape=outs,
            in_specs=[pl.BlockSpec(memory_space=pltpu.VMEM)] * len(operands),
            compiler_params=pltpu.CompilerParams(vmem_limit_bytes=limit),
            cost_estimate=pl.CostEstimate(
                flops=flops, bytes_accessed=flops, transcendentals=0
            ),
        )(*operands)

    def out(shape, kind=jnp.bfloat16):
        return jax.ShapeDtypeStruct(shape, kind)

    flat_inputs = decode_step_inputs.reshape(-1, own_width)

    sent = out((groups, own_rows, wide))
    masters = call(
        send_masters, sent, adapter_down_master, by_rank(adapter_up_master), limit=None
    )
    later_inputs = after(flat_inputs, masters)
    frozen_part = call(
        project_decode,
        out((ranks * own_lines, kinds * columns), jnp.float32),
        later_inputs,
        frozen_weights,
    )
    bits = ranks.bit_length() - 1
    frozen_part = frozen_part.reshape((2,) * bits + (own_lines, kinds * columns))
    factors = exchange(masters, "grp").reshape(all_rows, wide)

    frozen_part = half_sum(frozen_part, "tp", ranks, bits - 1, 0, earlier_sum=factors)
    frozen_part = half_sum(frozen_part, "tp", ranks, 1, bits - 2)

    lines = query_width // (head_groups * head_size) * own_lines
    query_lines = (
        after(queries, factors).reshape(row_count, steps_count, head_groups, -1, head_size)
        .transpose(2, 3, 0, 1, 4)
        .reshape(head_groups, lines, head_size)
    )
    column = jax.ShapeDtypeStruct((head_groups, lines, 1), jnp.float32)
    peak, total, cached = pl.pallas_call(
        cached_attention,
        out_shape=(
            column,
            column,
            jax.ShapeDtypeStruct((head_groups, lines, head_size), jnp.float32),
        ),
        in_specs=[pl.BlockSpec(memory_space=pltpu.SMEM)]
        + [pl.BlockSpec(memory_space=pltpu.VMEM)] * 3,
        compiler_params=pltpu.CompilerParams(vmem_limit_bytes=KERNEL_BYTES),
        cost_estimate=pl.CostEstimate(
            flops=8 * lines * cache_slots * head_size * head_groups,
            bytes_accessed=4 * row_count * head_groups * cache_slots * head_size,
            transcendentals=lines * cache_slots * head_groups,
        ),
    )(lengths, query_lines, rotated_key_cache, stored_value_cache)

    cotangents = weighted_output_cotangents.reshape(-1, tokens)
    shares = call(
        project_tokens, out((tokens, 2 * all_rows)), factors, trainer_token_inputs, cotangents
    ).reshape(ranks, -1, 2 * all_rows)
    sums = call(sum_tokens, out(shares.shape), exchange(shares, "tp"))
    sums, peak, total, cached = lax.optimization_barrier((sums, peak, total, cached))
    token_sums = exchange(sums, "tp").reshape(tokens, 2 * all_rows)

    gradients = call(
        functools.partial(send_gradients, own_rank=own_rank),
        sent,
        token_sums,
        trainer_token_inputs,
        cotangents,
    )
    own = out(adapter_down_master.shape, jnp.float32)
    small = out((own_rows, wide - own_width), jnp.float32)
    *fresh, fresh_factors = call(
        update_factors,
        (own, own, own, small, small, small, sent),
        exchange(gradients, "grp"),
        adapter_down_master,
        down_first_moment,
        down_second_moment,
        placed(adapter_up_master),
        placed(up_first_moment),
        placed(up_second_moment),
    )
    frozen_part = half_sum(
        frozen_part,
        "tp",
        ranks,
        1,
        1,
        earlier_sum=fresh_factors,
        earlier_send=gradients,
        kind=jnp.bfloat16,
    )
    frozen_sum = half_sum(frozen_part, "tp", ranks, 0, bits - 1)
    factors = exchange(fresh_factors, "grp").reshape(all_rows, wide)

    rank_space = call(
        functools.partial(send_rank_space, own_lines=own_lines),
        out((ranks, 2 * own_lines + own_columns, all_rows)),
        factors,
        flat_inputs,
    )

    positions = lengths[:, None] + jnp.arange(steps_count, dtype=jnp.int32)[None, :]
    angles = positions.astype(jnp.float32).reshape(-1, 1) * rope_frequencies(head_size)
    cosine, sine = jnp.cos(angles), jnp.sin(angles)
    cosine = jnp.concatenate([cosine, cosine], axis=1)
    sine = jnp.concatenate([-sine, sine], axis=1)

    rank_space, frozen_sum = lax.optimization_barrier((rank_space, frozen_sum))
    last = exchange(rank_space, "tp")
    entries = jax.ShapeDtypeStruct((row_count, steps_count, columns), jnp.float32)
    attended, new_keys, new_values = pl.pallas_call(
        functools.partial(finish, own_rank=own_rank),
        out_shape=(jax.ShapeDtypeStruct(queries.shape, jnp.float32), entries, entries),
        in_specs=[pl.BlockSpec(memory_space=pltpu.VMEM)] * 8,
        compiler_params=pltpu.CompilerParams(vmem_limit_bytes=KERNEL_BYTES),
        cost_estimate=pl.CostEstimate(
            flops=4 * lines * own_lines * head_size * head_groups,
            bytes_accessed=4 * queries.size,
            transcendentals=lines * own_lines * head_groups,
        ),
    )(last, frozen_sum, cosine, sine, query_lines, peak, total, cached)

    return (
        attended,
        new_keys,
        new_values,
        fresh[0],
        brought_back(fresh[3]),
        fresh[1],
        fresh[2],
        brought_back(fresh[4]),
        brought_back(fresh[5]),
    )


def solution(mesh):
    in_specs = (
        P("grp", "tp"),
        P(None, "tp", "grp"),
        P(None, "grp", "tp"),
        P(None, "tp", "grp"),
        P(None, "grp", "tp"),
        P(None, "grp", "tp"),
        P(None, "tp", "grp"),
        P(None, "tp", "grp"),
        P(None, "tp", None),
        P("grp", None, "tp"),
        P(("grp", "tp"), None, None),
        P(("grp", "tp"), None, None, None),
        P(("grp", "tp"), None, None, None),
        P(("grp", "tp")),
    )
    out_specs = (
        P(("grp", "tp"), None, None),
        P(("grp", "tp"), None, None),
        P(("grp", "tp"), None, None),
        P(None, "grp", "tp"),
        P(None, "tp", "grp"),
        P(None, "grp", "tp"),
        P(None, "grp", "tp"),
        P(None, "tp", "grp"),
        P(None, "tp", "grp"),
    )
    placed = functools.partial(body, mesh.shape["grp"], mesh.shape["tp"])
    return jax.shard_map(placed, mesh=mesh, in_specs=in_specs, out_specs=out_specs, check_vma=False)
```

```python
import functools
import math

import jax
import jax.numpy as jnp
from jax import lax
from jax.experimental import pallas as pl
from jax.experimental.pallas import tpu as pltpu
from jax.sharding import PartitionSpec as P

OPT_STEP = 20


ADAPTER_SCALE = 2.0
LEARN_RATE = 0.001
WEIGHT_DECAY = 0.01
BETA_FIRST = 0.9
BETA_SECOND = 0.95
EPSILON = 1e-08
THETA = 500000.0
ROPE_FACTOR = 8.0
LOW_FACTOR = 1.0
HIGH_FACTOR = 4.0
INITIAL_CONTEXT = 8192.0
MASKED = -1e30
KERNEL_BYTES = 8 * 1024 * 1024


def rope_frequencies(head_size):
    half_head = head_size // 2
    exponent = jnp.arange(half_head, dtype=jnp.float32) * (2.0 / head_size)
    base_frequency = jnp.power(jnp.float32(THETA), -exponent)
    wavelength = 2.0 * math.pi / base_frequency
    smooth = (INITIAL_CONTEXT / wavelength - LOW_FACTOR) / (HIGH_FACTOR - LOW_FACTOR)
    blended = (1.0 - smooth) * base_frequency / ROPE_FACTOR + smooth * base_frequency
    scaled = jnp.where(
        wavelength > INITIAL_CONTEXT / LOW_FACTOR, base_frequency / ROPE_FACTOR, blended
    )
    return jnp.where(wavelength < INITIAL_CONTEXT / HIGH_FACTOR, base_frequency, scaled)


def optimizer_update(current, gradient, moment_mean, moment_square):
    mean_next = BETA_FIRST * moment_mean + (1.0 - BETA_FIRST) * gradient
    square_next = BETA_SECOND * moment_square + (1.0 - BETA_SECOND) * gradient * gradient
    bias_first = 1.0 - BETA_FIRST**OPT_STEP
    bias_second = 1.0 - BETA_SECOND**OPT_STEP
    update = mean_next / bias_first / (jnp.sqrt(square_next / bias_second) + EPSILON)
    return (current - LEARN_RATE * (update + WEIGHT_DECAY * current), mean_next, square_next)


def exchange(pieces, axis):
    return lax.all_to_all(pieces, axis, 0, 0, tiled=True)


def product(spec, left, right):
    return jnp.einsum(spec, left, right, preferred_element_type=jnp.float32)


def after(values, earlier):
    return lax.optimization_barrier((values, earlier))[0]


def half_sum(values, axis, count, at, bit, earlier_sum=None, earlier_send=None, kind=jnp.float32):
    if earlier_send is not None:
        values = after(values, earlier_send)
    low = lax.index_in_dim(values, 0, at, keepdims=False)
    high = lax.index_in_dim(values, 1, at, keepdims=False)
    upper = (lax.axis_index(axis) >> bit) & 1 == 1
    pairs = [(place, place ^ (1 << bit)) for place in range(count)]
    arrived = lax.ppermute(jnp.where(upper, low, high).astype(kind), axis, pairs)
    kept = jnp.where(upper, high, low)
    if earlier_sum is not None:
        kept = after(kept, earlier_sum)
    return kept + arrived.astype(jnp.float32)


def dot_last(left, right):
    return lax.dot_general(
        left, right, (((1,), (1,)), ((), ())), preferred_element_type=jnp.float32
    )


def dot_first(left, right):
    return lax.dot_general(
        left, right, (((0,), (0,)), ((), ())), preferred_element_type=jnp.float32
    )


def kind_of_row(shape, own_rank):
    return lax.broadcasted_iota(jnp.int32, shape, 0) // own_rank % 2


def stack_kinds(ref):
    return jnp.concatenate([ref[0], ref[1]], axis=0)


def send_masters(down_ref, up_ref, out_ref):
    groups, _, wide = out_ref.shape
    own_rank, own_width = down_ref.shape[1:]
    own_columns = up_ref.shape[2]
    rest = wide - own_width
    rows = []
    for kind in range(2):
        line = up_ref[kind]
        before = jnp.zeros((own_rank, kind * own_columns), jnp.float32)
        after = jnp.zeros((own_rank, rest - (kind + 1) * own_columns), jnp.float32)
        parts = [part for part in (before, line, after) if part.shape[1]]
        rows.append(jnp.concatenate(parts, axis=1))
    block = jnp.concatenate([stack_kinds(down_ref), jnp.concatenate(rows, axis=0)], axis=1)
    block = block.astype(jnp.bfloat16)
    for group in range(groups):
        out_ref[group] = block


def project_decode(inputs_ref, weights_ref, out_ref):
    columns = weights_ref.shape[2]
    for kind in range(weights_ref.shape[0]):
        out_ref[:, kind * columns : (kind + 1) * columns] = jnp.dot(
            inputs_ref[...], weights_ref[kind], preferred_element_type=jnp.float32
        )


def project_tokens(factors_ref, inputs_ref, cotangents_ref, out_ref):
    all_rows = factors_ref.shape[0]
    own_width = inputs_ref.shape[1]
    both = cotangents_ref.shape[0]
    projected = dot_last(inputs_ref[...], factors_ref[:, :own_width])
    pulled = lax.dot_general(
        cotangents_ref[...],
        factors_ref[:, own_width : own_width + both],
        (((0,), (1,)), ((), ())),
        preferred_element_type=jnp.float32,
    )
    out_ref[:, :all_rows] = projected.astype(jnp.bfloat16)
    out_ref[:, all_rows:] = pulled.astype(jnp.bfloat16)


def sum_tokens(parts_ref, out_ref):
    total = jnp.sum(parts_ref[...].astype(jnp.float32), axis=0).astype(jnp.bfloat16)
    for rank in range(out_ref.shape[0]):
        out_ref[rank] = total


def send_gradients(tokens_ref, inputs_ref, cotangents_ref, out_ref, own_rank):
    groups, own_rows, wide = out_ref.shape
    all_rows = groups * own_rows
    own_width = inputs_ref.shape[1]
    both = cotangents_ref.shape[0]
    down = ADAPTER_SCALE * dot_first(tokens_ref[:, all_rows:], inputs_ref[...])
    cotangents = cotangents_ref[...]
    if wide - own_width > both:
        empty = jnp.zeros((wide - own_width - both, cotangents.shape[1]), jnp.bfloat16)
        cotangents = jnp.concatenate([cotangents, empty], axis=0)
    up = lax.dot_general(
        tokens_ref[:, :all_rows],
        cotangents,
        (((0,), (1,)), ((), ())),
        preferred_element_type=jnp.float32,
    )
    lane_kind = lax.broadcasted_iota(jnp.int32, up.shape, 1) // (both // 2)
    up = jnp.where(lane_kind == kind_of_row(up.shape, own_rank), ADAPTER_SCALE * up, 0.0)
    for group in range(groups):
        rows = slice(group * own_rows, (group + 1) * own_rows)
        out_ref[group, :, :own_width] = down[rows].astype(jnp.bfloat16)
        out_ref[group, :, own_width:] = up[rows].astype(jnp.bfloat16)


def update_factors(
    parts_ref,
    down_ref,
    down_first_ref,
    down_second_ref,
    up_ref,
    up_first_ref,
    up_second_ref,
    fresh_down_ref,
    fresh_down_first_ref,
    fresh_down_second_ref,
    fresh_up_ref,
    fresh_up_first_ref,
    fresh_up_second_ref,
    out_ref,
):
    groups = out_ref.shape[0]
    own_rank, own_width = down_ref.shape[1:]
    gradient = jnp.sum(parts_ref[...].astype(jnp.float32), axis=0)
    down = optimizer_update(
        stack_kinds(down_ref),
        gradient[:, :own_width],
        stack_kinds(down_first_ref),
        stack_kinds(down_second_ref),
    )
    up = optimizer_update(
        up_ref[...], gradient[:, own_width:], up_first_ref[...], up_second_ref[...]
    )
    for ref, values in zip(
        (fresh_down_ref, fresh_down_first_ref, fresh_down_second_ref), down
    ):
        for kind in range(2):
            ref[kind] = values[kind * own_rank : (kind + 1) * own_rank]
    for ref, values in zip((fresh_up_ref, fresh_up_first_ref, fresh_up_second_ref), up):
        ref[...] = values
    block = jnp.concatenate([down[0], up[0]], axis=1).astype(jnp.bfloat16)
    for group in range(groups):
        out_ref[group] = block


def send_rank_space(factors_ref, inputs_ref, out_ref, own_lines):
    ranks, height, _ = out_ref.shape
    own_columns = height - 2 * own_lines
    own_width = inputs_ref.shape[1]
    values = dot_last(inputs_ref[...], factors_ref[:, :own_width])
    high = values.astype(jnp.bfloat16).astype(jnp.float32)
    low = values - high
    up = factors_ref[:, own_width:].astype(jnp.float32).T
    up = (up[:own_columns] + up[own_columns : 2 * own_columns]).astype(jnp.bfloat16)
    for rank in range(ranks):
        rows = slice(rank * own_lines, (rank + 1) * own_lines)
        both = jnp.concatenate([high[rows], low[rows]], axis=0)
        out_ref[rank, : 2 * own_lines] = both.astype(jnp.bfloat16)
        out_ref[rank, 2 * own_lines :] = up


def cached_attention(lengths_ref, query_ref, key_ref, value_ref, peak_ref, total_ref, sum_ref):
    row_count, heads, slots, size = key_ref.shape
    lines = query_ref.shape[1]
    steps = 4
    line = lax.broadcasted_iota(jnp.int32, (lines, slots), 0) // steps % row_count
    slot = lax.broadcasted_iota(jnp.int32, (lines, slots), 1)
    valid = [(line == row) & (slot < lengths_ref[row]) for row in range(row_count)]
    for head in range(heads):
        query = query_ref[head]
        scores = jnp.full((lines, slots), MASKED, jnp.float32)
        for row in range(row_count):
            found = dot_last(query, key_ref[row, head]) * (1.0 / math.sqrt(size))
            scores = jnp.where(valid[row], found, scores)
        peak = jnp.max(scores, axis=1, keepdims=True)
        weights = jnp.exp(scores - peak)
        result = jnp.zeros((lines, size), jnp.float32)
        for row in range(row_count):
            own = jnp.where(valid[row], weights, 0.0).astype(jnp.bfloat16)
            result += jnp.dot(own, value_ref[row, head], preferred_element_type=jnp.float32)
        peak_ref[head] = peak
        total_ref[head] = jnp.sum(weights, axis=1, keepdims=True)
        sum_ref[head] = result


def finish(
    last_ref,
    frozen_ref,
    cosine_ref,
    sine_ref,
    query_ref,
    peak_ref,
    total_ref,
    sum_ref,
    attended_ref,
    keys_ref,
    values_ref,
    own_rank,
):
    row_count, steps, _ = keys_ref.shape
    heads, lines, size = query_ref.shape
    own_lines = row_count * steps
    ranks, _, all_rows = last_ref.shape
    parts = jnp.sum(last_ref[:, : 2 * own_lines, :].astype(jnp.float32), axis=0)
    rank_space = parts[:own_lines] + parts[own_lines:]
    full_up = last_ref[:, 2 * own_lines :, :].reshape(-1, all_rows)
    columns = full_up.shape[0]
    adapter_row = lax.broadcasted_iota(jnp.int32, (own_lines, all_rows), 1)
    raw = []
    for kind in range(2):
        own = jnp.where(adapter_row // own_rank % 2 == kind, rank_space, 0.0)
        high = own.astype(jnp.bfloat16).astype(jnp.float32)
        both = jnp.concatenate([high, own - high], axis=0).astype(jnp.bfloat16)
        both = dot_last(both, full_up)
        raw.append(
            frozen_ref[:, kind * columns : (kind + 1) * columns]
            + ADAPTER_SCALE * (both[:own_lines] + both[own_lines:])
        )
    for row in range(row_count):
        values_ref[row] = raw[1][row * steps : (row + 1) * steps]

    line = lax.broadcasted_iota(jnp.int32, (lines, 2 * own_lines), 0)
    entry = lax.broadcasted_iota(jnp.int32, (lines, 2 * own_lines), 1)
    valid = (line // steps % row_count == entry // steps) & (entry % steps <= line % steps)
    for head in range(heads):
        lanes = slice(head * size, (head + 1) * size)
        vector = raw[0][:, lanes]
        turned = pltpu.roll(vector, size // 2, 1)
        rotated = vector * cosine_ref[...] + turned * sine_ref[...]
        for row in range(row_count):
            keys_ref[row, :, lanes] = rotated[row * steps : (row + 1) * steps]
        fresh_keys = jnp.concatenate([rotated, rotated], axis=0).astype(jnp.bfloat16)
        fresh_values = jnp.concatenate([raw[1][:, lanes]] * 2, axis=0).astype(jnp.bfloat16)
        scores = dot_last(query_ref[head], fresh_keys) * (1.0 / math.sqrt(size))
        scores = jnp.where(valid, scores, MASKED)
        peak = jnp.maximum(peak_ref[head], jnp.max(scores, axis=1, keepdims=True))
        scale = jnp.exp(peak_ref[head] - peak)
        weights = jnp.where(valid, jnp.exp(scores - peak), 0.0)
        total = total_ref[head] * scale + jnp.sum(weights, axis=1, keepdims=True)
        result = sum_ref[head] * scale + jnp.dot(
            weights.astype(jnp.bfloat16), fresh_values, preferred_element_type=jnp.float32
        )
        result = result * (1.0 / total)
        group = lines // own_lines
        for query_head in range(group):
            at = (head * group + query_head) * size
            for row in range(row_count):
                start = query_head * own_lines + row * steps
                attended_ref[row, :, at : at + size] = result[start : start + steps]


def body(
    groups,
    ranks,
    trainer_token_inputs,
    weighted_output_cotangents,
    adapter_down_master,
    adapter_up_master,
    down_first_moment,
    down_second_moment,
    up_first_moment,
    up_second_moment,
    frozen_weights,
    decode_step_inputs,
    queries,
    rotated_key_cache,
    stored_value_cache,
    lengths,
):
    row_count, steps_count, query_width = queries.shape
    head_groups, cache_slots, head_size = rotated_key_cache.shape[1:]
    kinds, own_rank, own_width = adapter_down_master.shape
    own_columns, tokens = weighted_output_cotangents.shape[1:]
    columns = own_columns * ranks
    own_rows = kinds * own_rank
    all_rows = own_rows * groups
    own_lines = row_count * steps_count
    wide = own_width + -(-kinds * own_columns // 128) * 128

    def by_rank(values):
        return values.transpose(0, 2, 1)

    def placed(values):
        rest = wide - own_width - own_columns
        return jnp.concatenate(
            [
                jnp.pad(by_rank(values)[kind], ((0, 0), (at, rest - at)))
                for kind, at in ((0, 0), (1, own_columns))
            ]
        )

    def brought_back(values):
        blocks = [
            values[kind * own_rank : (kind + 1) * own_rank, at : at + own_columns]
            for kind, at in ((0, 0), (1, own_columns))
        ]
        return by_rank(jnp.stack(blocks))

    def call(kernel, outs, *operands, limit=KERNEL_BYTES):
        flops = 4 * max(operand.size for operand in operands)
        return pl.pallas_call(
            kernel,
            out_shape=outs,
            in_specs=[pl.BlockSpec(memory_space=pltpu.VMEM)] * len(operands),
            compiler_params=pltpu.CompilerParams(vmem_limit_bytes=limit),
            cost_estimate=pl.CostEstimate(
                flops=flops, bytes_accessed=flops, transcendentals=0
            ),
        )(*operands)

    def out(shape, kind=jnp.bfloat16):
        return jax.ShapeDtypeStruct(shape, kind)

    flat_inputs = decode_step_inputs.reshape(-1, own_width)

    sent = out((groups, own_rows, wide))
    masters = call(
        send_masters, sent, adapter_down_master, by_rank(adapter_up_master), limit=None
    )
    later_inputs = after(flat_inputs, masters)
    frozen_part = call(
        project_decode,
        out((ranks * own_lines, kinds * columns), jnp.float32),
        later_inputs,
        frozen_weights,
    )
    bits = ranks.bit_length() - 1
    frozen_part = frozen_part.reshape((2,) * bits + (own_lines, kinds * columns))
    factors = exchange(masters, "grp").reshape(all_rows, wide)

    frozen_part = half_sum(frozen_part, "tp", ranks, bits - 1, 0, earlier_sum=factors)
    frozen_part = half_sum(frozen_part, "tp", ranks, 1, bits - 2, kind=jnp.bfloat16)

    lines = query_width // (head_groups * head_size) * own_lines
    query_lines = (
        after(queries, factors).reshape(row_count, steps_count, head_groups, -1, head_size)
        .transpose(2, 3, 0, 1, 4)
        .reshape(head_groups, lines, head_size)
    )
    column = jax.ShapeDtypeStruct((head_groups, lines, 1), jnp.float32)
    peak, total, cached = pl.pallas_call(
        cached_attention,
        out_shape=(
            column,
            column,
            jax.ShapeDtypeStruct((head_groups, lines, head_size), jnp.float32),
        ),
        in_specs=[pl.BlockSpec(memory_space=pltpu.SMEM)]
        + [pl.BlockSpec(memory_space=pltpu.VMEM)] * 3,
        compiler_params=pltpu.CompilerParams(vmem_limit_bytes=KERNEL_BYTES),
        cost_estimate=pl.CostEstimate(
            flops=8 * lines * cache_slots * head_size * head_groups,
            bytes_accessed=4 * row_count * head_groups * cache_slots * head_size,
            transcendentals=lines * cache_slots * head_groups,
        ),
    )(lengths, query_lines, rotated_key_cache, stored_value_cache)

    cotangents = weighted_output_cotangents.reshape(-1, tokens)
    shares = call(
        project_tokens, out((tokens, 2 * all_rows)), factors, trainer_token_inputs, cotangents
    ).reshape(ranks, -1, 2 * all_rows)
    sums = call(sum_tokens, out(shares.shape), exchange(shares, "tp"))
    sums, peak, total, cached = lax.optimization_barrier((sums, peak, total, cached))
    token_sums = exchange(sums, "tp").reshape(tokens, 2 * all_rows)

    gradients = call(
        functools.partial(send_gradients, own_rank=own_rank),
        sent,
        token_sums,
        trainer_token_inputs,
        cotangents,
    )
    own = out(adapter_down_master.shape, jnp.float32)
    small = out((own_rows, wide - own_width), jnp.float32)
    *fresh, fresh_factors = call(
        update_factors,
        (own, own, own, small, small, small, sent),
        exchange(gradients, "grp"),
        adapter_down_master,
        down_first_moment,
        down_second_moment,
        placed(adapter_up_master),
        placed(up_first_moment),
        placed(up_second_moment),
    )
    frozen_part = half_sum(
        frozen_part,
        "tp",
        ranks,
        1,
        1,
        earlier_sum=fresh_factors,
        earlier_send=gradients,
        kind=jnp.bfloat16,
    )
    frozen_sum = half_sum(frozen_part, "tp", ranks, 0, bits - 1)
    factors = exchange(fresh_factors, "grp").reshape(all_rows, wide)

    rank_space = call(
        functools.partial(send_rank_space, own_lines=own_lines),
        out((ranks, 2 * own_lines + own_columns, all_rows)),
        factors,
        flat_inputs,
    )

    positions = lengths[:, None] + jnp.arange(steps_count, dtype=jnp.int32)[None, :]
    angles = positions.astype(jnp.float32).reshape(-1, 1) * rope_frequencies(head_size)
    cosine, sine = jnp.cos(angles), jnp.sin(angles)
    cosine = jnp.concatenate([cosine, cosine], axis=1)
    sine = jnp.concatenate([-sine, sine], axis=1)

    rank_space, frozen_sum = lax.optimization_barrier((rank_space, frozen_sum))
    last = exchange(rank_space, "tp")
    entries = jax.ShapeDtypeStruct((row_count, steps_count, columns), jnp.float32)
    attended, new_keys, new_values = pl.pallas_call(
        functools.partial(finish, own_rank=own_rank),
        out_shape=(jax.ShapeDtypeStruct(queries.shape, jnp.float32), entries, entries),
        in_specs=[pl.BlockSpec(memory_space=pltpu.VMEM)] * 8,
        compiler_params=pltpu.CompilerParams(vmem_limit_bytes=KERNEL_BYTES),
        cost_estimate=pl.CostEstimate(
            flops=4 * lines * own_lines * head_size * head_groups,
            bytes_accessed=4 * queries.size,
            transcendentals=lines * own_lines * head_groups,
        ),
    )(last, frozen_sum, cosine, sine, query_lines, peak, total, cached)

    return (
        attended,
        new_keys,
        new_values,
        fresh[0],
        brought_back(fresh[3]),
        fresh[1],
        fresh[2],
        brought_back(fresh[4]),
        brought_back(fresh[5]),
    )


def solution(mesh):
    in_specs = (
        P("grp", "tp"),
        P(None, "tp", "grp"),
        P(None, "grp", "tp"),
        P(None, "tp", "grp"),
        P(None, "grp", "tp"),
        P(None, "grp", "tp"),
        P(None, "tp", "grp"),
        P(None, "tp", "grp"),
        P(None, "tp", None),
        P("grp", None, "tp"),
        P(("grp", "tp"), None, None),
        P(("grp", "tp"), None, None, None),
        P(("grp", "tp"), None, None, None),
        P(("grp", "tp")),
    )
    out_specs = (
        P(("grp", "tp"), None, None),
        P(("grp", "tp"), None, None),
        P(("grp", "tp"), None, None),
        P(None, "grp", "tp"),
        P(None, "tp", "grp"),
        P(None, "grp", "tp"),
        P(None, "grp", "tp"),
        P(None, "tp", "grp"),
        P(None, "tp", "grp"),
    )
    placed = functools.partial(body, mesh.shape["grp"], mesh.shape["tp"])
    return jax.shard_map(placed, mesh=mesh, in_specs=in_specs, out_specs=out_specs, check_vma=False)
```
